256 devices in a mesh: row: 16 (over x, y_lo, core), col: 16 (over y_hi, z).
Axes of the slice: x: 4, y: 4 (y_hi: 2, y_lo: 2; y = y_hi * 2 + y_lo), z: 8, core: 2. Of those that a mesh axis runs over, the one named last changes fastest.
Arguments:
- queries: bfloat16 [1024, 192], P(('row', 'col')), may hold values from -12 to 12
- query_points: bfloat16 [1024, 144], P(('row', 'col')), may hold values from -4 to 4
- key_feats: bfloat16 [1024, 192], P(('col', 'row')), may hold values from -12 to 12
- key_points: bfloat16 [1024, 144], P(('col', 'row')), may hold values from -4 to 4
- values: bfloat16 [1024, 192], P(('col', 'row')), may hold values from -5 to 5
- value_points: bfloat16 [1024, 288], P(('col', 'row')), may hold values from -5 to 5
- pair_rep: float32 [1024, 1024, 128], P('row', 'col'), may hold values from -6 to 6
- bias_weight: float32 [128, 12], replicated, may hold values from -0.5 to 0.5
- head_weight: float32 [12], replicated, may hold values from 0.1 to 1
- chain_bias: float32 [12], replicated, may hold values from -3 to 3
- chain_ids: int32 [1024], replicated, may hold values from 0 to 7, never falling along the last dimension, each value on 1 to 256 neighbouring positions
- live_mask: int32 [1024], replicated, may hold values from 0 to 1, as said below
- cot_scalar: bfloat16 [1024, 192], P(('row', 'col')), may hold values from -5 to 5
- cot_points: bfloat16 [1024, 288], P(('row', 'col')), may hold values from -5 to 5
- cot_pair: bfloat16 [1024, 1536], P(('row', 'col')), may hold values from -5 to 5
Outputs:
- grad_queries: float32 [1024, 192], P(('row', 'col'))
- grad_query_points: float32 [1024, 144], P(('row', 'col'))
- grad_keys: float32 [1024, 192], P(('col', 'row'))
- grad_key_points: float32 [1024, 144], P(('col', 'row'))
- grad_values: float32 [1024, 192], P(('col', 'row'))
- grad_value_points: float32 [1024, 288], P(('col', 'row'))
- grad_pair: float32 [1024, 1024, 128], P('row', 'col')
- grad_bias_weight: float32 [128, 12], replicated
The draws below stay inside these ranges and needn't reach their ends.
Inputs may be any that keep to these rules, and one draw needn't show every extreme that they name: `live_mask`: at least one residue is live.
All inputs are finite; a program needn't handle non-finite values.
Results may differ from the reference program's by a relative error of at most 0.0175.
Values may be sent and summed in bfloat16 or wider, within the bound.
A program may use at most 64 MiB of HBM per device.

```python
import math
import jax
import jax.numpy as jnp
import numpy as np
from jax import lax

H = 12
C = 16
PQ = 4
PV = 8
CZ = 128
N = 1024
N_ROW = 16


def draw_queries(key, part):
    key = jax.random.fold_in(key, 1)
    drawn = jnp.clip(jax.random.normal(key, (N, H * C), jnp.float32), -4.0, 4.0)
    return drawn.astype(jnp.bfloat16)


def draw_key_feats(key, part):
    key = jax.random.fold_in(key, 2)
    drawn = jnp.clip(jax.random.normal(key, (N, H * C), jnp.float32), -4.0, 4.0)
    return drawn.astype(jnp.bfloat16)


def draw_live_mask(key, part):
    key = jax.random.fold_in(key, 5)
    levels = jax.random.randint(key, (N,), 0, 8)
    chosen = jax.random.randint(jax.random.fold_in(key, 1), (), 0, N)
    live = (levels != 0) | (jnp.arange(N, dtype=jnp.int32) == chosen)
    return live.astype(jnp.int32)


def level_of(own_key, dims, pieces, least, high):
    loudness, own = 1.0, jax.random.fold_in(own_key, 6)
    for position, parts in pieces:
        draws = jnp.exp(jax.random.uniform(jax.random.fold_in(own, position), (parts,), jnp.float32, least / len(pieces), high / len(pieces)))
        loudness = loudness * jnp.repeat(draws, dims[position] // parts).reshape([-1 if axis == position else 1 for axis in range(len(dims))])
    return loudness


def profile(count, total, reach, lean):
    portions = [(1 << 20) // math.isqrt(grade ** lean) + 1 for grade in range(2, count + 1)]
    spare, given = total - reach - (count - 1), [1] * (count - 1)
    while spare > 0:
        movable = [i for i in range(count - 1) if given[i] < reach]
        mass, remaining = sum([portions[i] for i in movable]), spare
        for i in movable:
            more = min(reach - given[i], max(1, remaining * portions[i] // mass), spare)
            given[i] = given[i] + more
            spare = spare - more
    return np.array([reach] + given)


def uneven_parts(own_key, number_of, total, limit, skew):
    if number_of == 2:
        one = jax.random.randint(own_key, (), max(1, total - limit), min(limit, total - 1) + 1)
        return jnp.stack([one, total - one])
    sizes = jnp.asarray(profile(number_of, total, limit, skew), jnp.int32)
    twos = (number_of - 1) // 2
    donor, taker = sizes[1:1 + 2 * twos:2], sizes[2:2 + 2 * twos:2]
    margin = jnp.minimum(donor - 1, limit - taker)
    moved = jax.random.randint(jax.random.fold_in(own_key, 1), (twos,), 0, 1 << 20) % (margin + 1)
    sizes = sizes.at[1:1 + 2 * twos:2].set(donor - moved).at[2:2 + 2 * twos:2].set(taker + moved)
    return sizes[jax.random.permutation(jax.random.fold_in(own_key, 2), number_of)]


def centred(own_key, dims, scale, limit, shards=(), kind=jnp.bfloat16):
    loudness = level_of(own_key, dims, shards, -0.22, 0.18) if shards else 1.0
    values = jax.random.normal(own_key, dims, jnp.float32) * scale * loudness
    return jnp.minimum(jnp.maximum(values, -limit), limit).astype(kind)


def setup_inputs(seed: int = 0) -> dict:
    key_list = jax.random.split(jax.random.key(seed), 16)
    return {
        "queries": draw_queries(jax.random.fold_in(key_list[15], 71), 0),
        "query_points": centred(key_list[1], (N, 3 * H * PQ), 1.0, 4.0, ((0, 256),)),
        "key_feats": draw_key_feats(jax.random.fold_in(key_list[15], 71), 0),
        "key_points": centred(key_list[3], (N, 3 * H * PQ), 1.0, 4.0, ((0, 256),)),
        "values": centred(key_list[4], (N, H * C), 1.0, 5.0, ((0, 256),)),
        "value_points": centred(key_list[5], (N, 3 * H * PV), 1.0, 5.0, ((0, 256),)),
        "pair_rep": centred(key_list[6], (N, N, CZ), 1.0, 6.0, ((0, 16), (1, 16)), jnp.float32),
        "bias_weight": centred(key_list[7], (CZ, H), CZ ** -0.5, 0.5, (), jnp.float32),
        "head_weight": jnp.clip(jnp.exp(jax.random.uniform(key_list[8], (H,), jnp.float32, math.log(0.1), math.log(1.0))), 0.1, 1.0),
        "chain_bias": jnp.clip(jax.random.uniform(key_list[9], (H,), jnp.float32, -3.0, 3.0), -3.0, 3.0),
        "chain_ids": jnp.searchsorted(jnp.cumsum(uneven_parts(key_list[10], 8, N, N // 4, 0)), jnp.arange(N), side="right").astype(jnp.int32),
        "live_mask": draw_live_mask(jax.random.fold_in(key_list[15], 71), 0),
        "cot_scalar": centred(key_list[12], (N, H * C), 1.0, 5.0, ((0, 256),)),
        "cot_points": centred(key_list[13], (N, 3 * H * PV), 1.0, 5.0, ((0, 256),)),
        "cot_pair": centred(key_list[14], (N, H * CZ), 1.0, 5.0, ((0, 256),)),
    }


HIGH = lax.Precision.HIGHEST
NEG_FILL = -1e+30

def reference(queries, query_points, key_feats, key_points, values, value_points, pair_rep, bias_weight, head_weight, chain_bias, chain_ids, live_mask, cot_scalar, cot_points, cot_pair):
    num_heads = head_weight.shape[0]
    head_size = queries.shape[1] // num_heads
    residues = queries.shape[0]
    channels = bias_weight.shape[0]
    block_rows = residues // N_ROW
    w_logit = math.sqrt(1.0 / 3.0)
    w_point = math.sqrt(2.0 / (9.0 * PQ))
    point_scale = w_logit * head_weight * w_point / 2.0
    scale_q = w_logit / math.sqrt(head_size)
    key_f = key_feats.astype(jnp.float32).reshape(residues, num_heads, head_size)
    kpt_f = key_points.astype(jnp.float32).reshape(residues, num_heads, 3 * PQ)
    val_f = values.astype(jnp.float32).reshape(residues, num_heads, head_size)
    vpt_f = value_points.astype(jnp.float32).reshape(residues, num_heads, 3 * PV)
    k_sq = lax.optimization_barrier(jnp.sum(kpt_f * kpt_f, -1)).T
    live_k = live_mask.astype(jnp.float32)

    def one_block(carry, index):
        acc_k, acc_kp, acc_v, acc_vp, acc_w = carry
        begin = index * block_rows

        def take_rows(array):
            return lax.dynamic_slice_in_dim(array, begin, block_rows, 0)
        live_q = take_rows(live_mask).astype(jnp.bfloat16)
        q_f = take_rows(queries).astype(jnp.float32).reshape(block_rows, num_heads, head_size)
        qpt_f = take_rows(query_points).astype(jnp.float32).reshape(block_rows, num_heads, 3 * PQ)
        gsc_f = (take_rows(cot_scalar) * live_q[:, None]).astype(jnp.float32).reshape(block_rows, num_heads, head_size)
        gpt_f = (take_rows(cot_points) * live_q[:, None]).astype(jnp.float32).reshape(block_rows, num_heads, 3 * PV)
        gpr_f = (take_rows(cot_pair) * live_q[:, None]).astype(jnp.float32).reshape(block_rows, num_heads, channels)
        pair_rows = take_rows(pair_rep)
        chain_q = take_rows(chain_ids)
        q_sq = lax.optimization_barrier(jnp.sum(qpt_f * qpt_f, -1)).T
        scalar_dot = jnp.einsum('ihc,jhc->hij', q_f, key_f, precision=HIGH)
        point_dot = jnp.einsum('ihd,jhd->hij', qpt_f, kpt_f, precision=HIGH)
        distance = q_sq[:, :, None] + k_sq[:, None, :] - 2.0 * point_dot
        pair_bias = jnp.einsum('ijc,ch->hij', pair_rows, bias_weight, precision=HIGH)
        same_chain = (chain_q[:, None] == chain_ids[None, :]).astype(jnp.float32)
        logits = w_logit * (scalar_dot / math.sqrt(head_size) + pair_bias + chain_bias[:, None, None] * same_chain) - point_scale[:, None, None] * distance
        logits = jnp.where(live_k[None, None, :] > 0, logits, NEG_FILL)
        row_max = lax.optimization_barrier(jnp.max(logits, -1, keepdims=True))
        expo = jnp.exp(logits - row_max) * live_k[None, None, :]
        prob = expo / lax.optimization_barrier(jnp.sum(expo, -1, keepdims=True))
        prob16 = lax.optimization_barrier(prob.astype(jnp.bfloat16)).astype(jnp.float32)
        dprob = jnp.einsum('ihc,jhc->hij', gsc_f, val_f, precision=HIGH)
        dprob = dprob + jnp.einsum('ihd,jhd->hij', gpt_f, vpt_f, precision=HIGH)
        dprob = dprob + jnp.einsum('ihc,ijc->hij', gpr_f, pair_rows, precision=HIGH)
        dsum = lax.optimization_barrier(jnp.sum(prob * dprob, -1, keepdims=True))
        dscore = prob * (dprob - dsum)
        ds16 = lax.optimization_barrier(dscore.astype(jnp.bfloat16)).astype(jnp.float32)
        grad_q = scale_q * jnp.einsum('hij,jhc->ihc', ds16, key_f, precision=HIGH)
        row_sums = lax.optimization_barrier(jnp.sum(ds16, -1)).T
        grad_qp = -2.0 * point_scale[None, :, None] * (row_sums[:, :, None] * qpt_f - jnp.einsum('hij,jhd->ihd', ds16, kpt_f, precision=HIGH))
        col_sums = lax.optimization_barrier(jnp.sum(ds16, 1)).T
        acc_k = acc_k + scale_q * jnp.einsum('hij,ihc->jhc', ds16, q_f, precision=HIGH)
        acc_kp = acc_kp - 2.0 * point_scale[None, :, None] * (col_sums[:, :, None] * kpt_f - jnp.einsum('hij,ihd->jhd', ds16, qpt_f, precision=HIGH))
        acc_v = acc_v + jnp.einsum('hij,ihc->jhc', prob16, gsc_f, precision=HIGH)
        acc_vp = acc_vp + jnp.einsum('hij,ihd->jhd', prob16, gpt_f, precision=HIGH)
        acc_w = acc_w + w_logit * jnp.einsum('ijc,hij->ch', pair_rows, dscore, precision=HIGH)
        grad_tile = jnp.einsum('hij,ihc->ijc', prob16, gpr_f, precision=HIGH) + w_logit * jnp.einsum('hij,ch->ijc', dscore, bias_weight, precision=HIGH)
        return ((acc_k, acc_kp, acc_v, acc_vp, acc_w), (grad_q.reshape(block_rows, -1), grad_qp.reshape(block_rows, -1), grad_tile))
    init = (jnp.zeros((residues, num_heads, head_size), jnp.float32), jnp.zeros((residues, num_heads, 3 * PQ), jnp.float32), jnp.zeros((residues, num_heads, head_size), jnp.float32), jnp.zeros((residues, num_heads, 3 * PV), jnp.float32), jnp.zeros((channels, num_heads), jnp.float32))
    carry, stacked = lax.scan(one_block, init, jnp.arange(N_ROW, dtype=jnp.int32))
    acc_k, acc_kp, acc_v, acc_vp, acc_w = carry
    grad_queries = stacked[0].reshape(residues, -1)
    grad_query_points = stacked[1].reshape(residues, -1)
    grad_pair = stacked[2].reshape(residues, residues, channels)
    return (grad_queries, grad_query_points, acc_k.reshape(residues, -1), acc_kp.reshape(residues, -1), acc_v.reshape(residues, -1), acc_vp.reshape(residues, -1), grad_pair, acc_w)
```

```python
import math

import jax
import jax.numpy as jnp
from jax import lax
from jax.experimental import pallas as pl
from jax.experimental.pallas import tpu as pltpu
from jax.sharding import PartitionSpec as P

MESH = pl.DeviceIdType.MESH
NEG_FILL = -1e30
F32 = jnp.float32
BF16 = jnp.bfloat16
H = 12
HP = 16
TILE = 64
PEERS = 16
W_LOGIT = math.sqrt(1.0 / 3.0)
W_POINT = math.sqrt(2.0 / 36.0)
SCALE_Q = W_LOGIT / 4.0


def nt(a, b):
    return lax.dot_general(a, b, (((1,), (1,)), ((), ())), preferred_element_type=F32)


def nn(a, b):
    return lax.dot_general(a, b, (((1,), (0,)), ((), ())), preferred_element_type=F32)


def tn(a, b):
    return lax.dot_general(a, b, (((0,), (0,)), ((), ())), preferred_element_type=F32)


def exact_nn(a, b):
    return lax.dot_general(
        a, b, (((1,), (0,)), ((), ())), preferred_element_type=F32, precision=lax.Precision.HIGHEST
    )


def split(x):
    high = x.astype(BF16)
    return high, (x - high.astype(F32)).astype(BF16)


def head_masks(sub, lane):
    def block(col, width):
        return (col >= sub * width) & (col < sub * width + width)

    tiles = [
        block(lane, 16),
        ((lane < 64) & block(lane + 128, 16)) | (lane == sub + 64) | (lane == sub + 80),
        block(lane, 12),
        (lane < 16) & block(lane + 128, 12),
        block(lane, 16),
        block(lane, 24),
        block(lane + 128, 24),
        ((lane < 64) & block(lane + 128, 16)) | ((lane >= 64) & (lane < 96) & block(lane + 192, 24)),
    ]
    return [(tile & (sub < H)).astype(F32) for tile in tiles]


def kernel(
    q_in, qp_in, k_in, kp_in, v_in, vp_in, pair_in, bw_in, hw_in, cb_in, chain_in, live_in,
    gs_in, gp_in, gz_in,
    gq_out, gqp_out, gk_out, gkp_out, gv_out, gvp_out, gpair_out, gbw_out,
    q_v, qp_v, k_v, kp_v, v_v, vp_v, pair_v, bw_v, hw_s, cb_s, chain_s, live_s, chain_v, live_v,
    gs_v, gp_v, gz_v,
    pack, gz32, qsend, ksend, gzsend, qg, kg, gzg, blk,
    qf, kf, kdup, qbd, kbd, pp, base, qsq, expo, dprob, prob, dsr, dlo,
    stats, stat_send, stat_g, w_send, w_row, w_mid, w_col,
    kres, kch, kr, qres, qch, qr,
    in_sem, out_sem, send_sem, recv_sem,
):
    r = lax.axis_index("row")
    c = lax.axis_index("col")
    barrier = pltpu.get_barrier_semaphore()

    @pl.loop(1, PEERS)
    def _(s):
        pl.semaphore_signal(barrier, inc=1, device_id=(r, lax.rem(c + s, PEERS)), device_id_type=MESH)
        pl.semaphore_signal(barrier, inc=1, device_id=(lax.rem(r + s, PEERS), c), device_id_type=MESH)

    loads = [
        pltpu.make_async_copy(src, dst, in_sem.at[n])
        for n, (src, dst) in enumerate(
            (
                (pair_in, pair_v), (q_in, q_v), (qp_in, qp_v), (k_in, k_v), (kp_in, kp_v), (v_in, v_v),
                (vp_in, vp_v), (bw_in, bw_v), (hw_in, hw_s), (cb_in, cb_s), (chain_in, chain_s),
                (live_in, live_s), (chain_in, chain_v), (live_in, live_v), (gs_in, gs_v), (gp_in, gp_v),
                (gz_in, gz_v),
            )
        )
    ]
    for load in loads[1:]:
        load.start()
    loads[0].start()
    for load in loads[1:]:
        load.wait()

    sub = lax.broadcasted_iota(jnp.int32, (HP, 128), 0)
    lane = lax.broadcasted_iota(jnp.int32, (HP, 128), 1)
    left = lane < 64
    masks = head_masks(sub, lane)

    live4 = jnp.zeros((4, 128), F32)
    sub4 = lax.broadcasted_iota(jnp.int32, (4, 128), 0)
    first = r * TILE + c * 4
    for i in range(4):
        at = first + i
        live4 = jnp.where(sub4 == i, live_s[at // 128, lax.rem(at, 128)].astype(F32), live4)

    def pack_block(scalars, points, vals, vpoints, ones, live, send):
        pack[...] = jnp.zeros_like(pack)
        a, b = scalars[...].astype(F32), points[...].astype(F32)
        d, e = vals[...].astype(F32), vpoints[...].astype(F32)
        pack[0:4, :] = a[:, 0:128]
        pack[4:8, 0:64] = a[:, 128:192]
        pack[4:8, ones : ones + 16] = jnp.ones((4, 16), F32)
        pack[8:12, :] = b[:, 0:128]
        pack[12:16, 0:16] = b[:, 128:144]
        pack[16:20, :] = d[:, 0:128] * live
        pack[20:24, :] = e[:, 0:128] * live
        pack[24:28, :] = e[:, 128:256] * live
        pack[28:32, 0:64] = d[:, 128:192] * live[:, 0:64]
        pack[28:32, 64:96] = e[:, 256:288] * live[:, 0:32]
        send[...] = pack[...].astype(BF16)

    pack_block(q_v, qp_v, gs_v, gp_v, 64, live4, qsend)
    pack_block(k_v, kp_v, v_v, vp_v, 80, jnp.ones((4, 128), F32), ksend)
    gz32[...] = jnp.zeros_like(gz32)
    for h in range(H):
        gz32[pl.ds(h, 4, stride=HP), :] = gz_v[:, 128 * h : 128 * h + 128].astype(F32) * live4
    gzsend[...] = gz32[...].astype(BF16)
    qg[c] = qsend[...]
    kg[r] = ksend[...]
    gzg[c] = gzsend[...]

    ps = jnp.zeros((HP, 128), F32)
    cb = jnp.zeros((HP, 128), F32)
    for h in range(H):
        ps = jnp.where(sub == h, hw_s[h], ps)
        cb = jnp.where(sub == h, cb_s[h], cb)
    ps = W_LOGIT * ps * W_POINT / 2.0
    ps_lane = [jnp.sum(masks[t] * ps, 0, keepdims=True) for t in (2, 3)]
    bw_pad = jnp.concatenate((bw_v[...], jnp.zeros((128, 128 - H), F32)), 1)
    bw_t = jnp.transpose(bw_pad)[0:HP, :]
    bw_high, bw_low = split(bw_t)
    wb_high, wb_low = split(W_LOGIT * bw_t)
    col_at = c * TILE
    chain_k = chain_v[pl.ds(col_at // 128, 1), :]
    live_k = live_v[pl.ds(col_at // 128, 1), :].astype(F32)
    half = lax.rem(c, 2)
    lane1 = lax.broadcasted_iota(jnp.int32, (1, 128), 1)
    own = (lane1 // 64) == half
    chain_k = jnp.where(own, chain_k, pltpu.roll(chain_k, 64, 1))
    live_k = jnp.where(own, live_k, pltpu.roll(live_k, 64, 1))

    loads[0].wait()
    bias_lhs = jnp.concatenate(
        (jnp.concatenate((bw_high, bw_high), 1), jnp.concatenate((bw_low, bw_low), 1)), 0
    )

    @pl.loop(0, 16)
    def _(t):
        high, low = split(pair_v[pl.ds(256 * t, 256), :])
        both = jnp.concatenate((high, low), 1)
        pp[pl.ds(256 * t, 256), :] = both
        res = nt(bias_lhs, both)
        res = res[0:HP] + res[HP : 2 * HP]
        for a in range(2):
            at = r * TILE + 4 * t + 2 * a
            chain_q = jnp.where(
                lane1 < 64, chain_s[at // 128, lax.rem(at, 128)], chain_s[(at + 1) // 128, lax.rem(at + 1, 128)]
            )
            same = (chain_q == chain_k).astype(F32)
            base[pl.ds(32 * t + 16 * a, 16), :] = W_LOGIT * (res[:, 128 * a : 128 * a + 128] + cb * same)

    pl.semaphore_wait(barrier, 2 * (PEERS - 1))

    def spread(src, dst, axis, n):
        me = c if axis == "col" else r

        @pl.loop(1, PEERS)
        def _(s):
            to = lax.rem(me + s, PEERS)
            pltpu.make_async_remote_copy(
                src_ref=src,
                dst_ref=dst.at[me],
                send_sem=send_sem.at[n],
                recv_sem=recv_sem.at[n],
                device_id=(r, to) if axis == "col" else (to, c),
                device_id_type=MESH,
            ).start()

    def scatter(src, dst, axis, n):
        me = c if axis == "col" else r

        @pl.loop(1, PEERS)
        def _(s):
            to = lax.rem(me + s, PEERS)
            pltpu.make_async_remote_copy(
                src_ref=src.at[to],
                dst_ref=dst.at[me],
                send_sem=send_sem.at[n],
                recv_sem=recv_sem.at[n],
                device_id=(r, to) if axis == "col" else (to, c),
                device_id_type=MESH,
            ).start()

    def wait_recv(dst, n):
        part = dst.at[pl.ds(0, PEERS - 1)]
        pltpu.make_async_copy(part, part, recv_sem.at[n]).wait()

    def wait_send(dst, n):
        part = dst.at[pl.ds(0, PEERS - 1)]
        pltpu.make_async_copy(part, part, send_sem.at[n]).wait()

    spread(qsend, qg, "col", 0)
    spread(ksend, kg, "row", 1)
    spread(gzsend, gzg, "col", 2)

    def assemble(got, full):
        blk[...] = got[...].astype(F32)
        for s in range(PEERS):
            for t in range(8):
                full[4 * s : 4 * s + 4, 128 * t : 128 * t + 128] = blk[s, 4 * t : 4 * t + 4, :]

    wait_recv(kg, 1)
    assemble(kg, kf)
    kb = kf[...].astype(BF16)
    kdup[0:TILE, :] = kb
    kdup[TILE : 2 * TILE, :] = kb
    for h in range(H):
        for t in range(4):
            kbd[TILE * h : TILE * h + TILE, 128 * t : 128 * t + 128] = (
                kf[:, 128 * t : 128 * t + 128] * masks[t][h : h + 1, :]
            ).astype(BF16)
    kp_sq_high, kp_sq_low = split(kf[:, 256:512] * kf[:, 256:512])
    point_mask = jnp.concatenate((masks[2], masks[3]), 1)
    point_mask16 = point_mask.astype(BF16)
    k_sq = nt(point_mask16, kp_sq_high) + nt(point_mask16, kp_sq_low)
    k_sq = jnp.concatenate((k_sq, k_sq), 1)

    wait_recv(qg, 0)
    assemble(qg, qf)

    @pl.loop(0, 8)
    def _(b):
        eight = qf[pl.ds(pl.multiple_of(8 * b, 8), 8), :]
        for p in range(4):
            rows = pl.ds(64 * b + HP * p, HP)
            sums = []
            for odd in range(2):
                square = jnp.zeros((HP, 128), F32)
                for t in range(8):
                    value = eight[2 * p + odd : 2 * p + odd + 1, 128 * t : 128 * t + 128] * masks[t]
                    qbd[odd, rows, 128 * t : 128 * t + 128] = value.astype(BF16)
                    if t in (2, 3):
                        square = square + value * value
                sums.append(jnp.sum(square, 1, keepdims=True))
            qsq[rows, :] = jnp.where(left, sums[0], sums[1])

    stats[...] = jnp.zeros_like(stats)
    lane3 = lax.broadcasted_iota(jnp.int32, (8, HP, 128), 2)
    left3 = lane3 < 64

    @pl.loop(0, 4)
    def _(b):
        rows = pl.ds(128 * b, 128)
        parts = []
        for k0, k1 in ((0, 256), (256, 512), (512, 1024)):
            even = nt(qbd[0, rows, k0:k1], kdup[:, k0:k1]).reshape(8, HP, 128)
            odd = nt(qbd[1, rows, k0:k1], kdup[:, k0:k1]).reshape(8, HP, 128)
            parts.append(jnp.where(left3, even, odd))
        dprob[rows, :] = parts[2].reshape(128, 128)
        distance = qsq[rows, :].reshape(8, HP, 128) + k_sq - 2.0 * parts[1]
        logits = base[rows, :].reshape(8, HP, 128) + SCALE_Q * parts[0] - ps * distance
        logits = jnp.where(live_k > 0, logits, NEG_FILL)
        max0 = jnp.max(jnp.where(left3, logits, NEG_FILL), 2, keepdims=True)
        max1 = jnp.max(jnp.where(left3, NEG_FILL, logits), 2, keepdims=True)
        e = jnp.exp(logits - jnp.where(left3, max0, max1)) * live_k
        sum0 = jnp.sum(jnp.where(left3, e, 0.0), 2, keepdims=True)
        sum1 = jnp.sum(jnp.where(left3, 0.0, e), 2, keepdims=True)
        expo[rows, :] = e.reshape(128, 128)
        acc_m, acc_s = stats[0], stats[1]
        for i in range(8):
            at = 16 * b + 2 * i
            acc_m = jnp.where(lane == at, max0[i], jnp.where(lane == at + 1, max1[i], acc_m))
            acc_s = jnp.where(lane == at, sum0[i], jnp.where(lane == at + 1, sum1[i], acc_s))
        stats[0] = acc_m
        stats[1] = acc_s

    wait_recv(gzg, 2)

    @pl.loop(0, 16)
    def _(t):
        gz = gzg[t]
        res = nt(jnp.concatenate((gz, gz), 1), pp[pl.ds(256 * t, 256), :])
        acc = stats[2]
        for a in range(2):
            rows = pl.ds(32 * t + 16 * a, 16)
            tile = res[32 * a : 32 * a + 32, 128 * a : 128 * a + 128]
            value = dprob[rows, :] + jnp.where(left, tile[0:16], tile[16:32])
            dprob[rows, :] = value
            weighted = expo[rows, :] * value
            sum0 = jnp.sum(jnp.where(left, weighted, 0.0), 1, keepdims=True)
            sum1 = jnp.sum(jnp.where(left, 0.0, weighted), 1, keepdims=True)
            at = 4 * t + 2 * a
            acc = jnp.where(lane == at, sum0, jnp.where(lane == at + 1, sum1, acc))
        stats[2] = acc

    row_max, row_sum = stats[0], stats[1]
    any_live = row_sum > 0
    safe = jnp.where(any_live, row_sum, 1.0)
    lse = jnp.where(any_live, row_max + jnp.log(safe), NEG_FILL)
    mean = jnp.where(any_live, stats[2] / safe, 0.0)
    stat_send[...] = jnp.where(left, lse, pltpu.roll(mean, 64, 1))
    stat_g[c] = stat_send[...]
    spread(stat_send, stat_g, "col", 3)
    wait_recv(stat_g, 3)
    top = stat_g[0]
    for s in range(1, PEERS):
        top = jnp.maximum(top, stat_g[s])
    total = jnp.zeros((HP, 128), F32)
    dsum = jnp.zeros((HP, 128), F32)
    for s in range(PEERS):
        got = stat_g[s]
        weight = jnp.exp(got - top)
        total = total + weight
        dsum = dsum + weight * pltpu.roll(got, 64, 1)
    stats[0] = jnp.exp(row_max - top) / total
    stats[1] = dsum / total

    @pl.loop(0, 8)
    def _(b):
        scale = pltpu.roll(stats[0], lax.rem(128 - 8 * b, 128), 1)
        mean_all = pltpu.roll(stats[1], lax.rem(128 - 8 * b, 128), 1)
        for i in range(4):
            rows = pl.ds(64 * b + 16 * i, 16)
            factor = jnp.where(left, scale[:, 2 * i : 2 * i + 1], scale[:, 2 * i + 1 : 2 * i + 2])
            shift = jnp.where(left, mean_all[:, 2 * i : 2 * i + 1], mean_all[:, 2 * i + 1 : 2 * i + 2])
            p = expo[rows, :] * factor
            ds = p * (dprob[rows, :] - shift)
            high, low = split(ds)
            prob[rows, :] = p.astype(BF16).astype(F32)
            dsr[rows, :] = high.astype(F32)
            dlo[rows, :] = low

    def weight_step(t, acc):
        high = dsr[pl.ds(32 * t, 32), :].astype(BF16)
        low = dlo[pl.ds(32 * t, 32), :]
        lhs = jnp.concatenate(
            (
                jnp.concatenate((high[0:16], high[16:32]), 1),
                jnp.concatenate((low[0:16], low[16:32]), 1),
            ),
            0,
        )
        return acc + nn(lhs, pp[pl.ds(256 * t, 256), :])

    w_all = lax.fori_loop(0, 16, weight_step, jnp.zeros((2 * HP, 256), F32))
    w_all = w_all[:, 0:128] + w_all[:, 128:256]
    w_send[...] = W_LOGIT * (w_all[0:HP] + w_all[HP : 2 * HP])
    w_row[r] = w_send[...]
    spread(w_send, w_row, "row", 4)

    ds_t = jnp.transpose(dsr[...]).astype(BF16)
    prob_t = jnp.transpose(prob[...]).astype(BF16)
    kside = nn(ds_t[0:TILE], qbd[0, :, 0:512]) + nn(ds_t[TILE : 2 * TILE], qbd[1, :, 0:512])
    vside = nn(prob_t[0:TILE], qbd[0, :, 512:1024]) + nn(prob_t[TILE : 2 * TILE], qbd[1, :, 512:1024])
    expand_q = jnp.concatenate((jnp.zeros((64, 256), F32), point_mask, jnp.zeros((48, 256), F32)), 0)
    expand_k = jnp.concatenate((jnp.zeros((80, 256), F32), point_mask, jnp.zeros((32, 256), F32)), 0)
    ps_row = jnp.concatenate(ps_lane, 1)
    kres[:, 0:256] = SCALE_Q * kside[:, 0:256]
    kres[:, 256:512] = -2.0 * ps_row * (
        exact_nn(kside[:, 128:256], expand_q) * kf[:, 256:512] - kside[:, 256:512]
    )
    kres[:, 512:1024] = vside
    for s in range(PEERS):
        for t in range(8):
            kch[s, 4 * t : 4 * t + 4, :] = kres[4 * s : 4 * s + 4, 128 * t : 128 * t + 128]
    kr[r] = kch[r]
    scatter(kch, kr, "row", 5)

    left32 = lax.broadcasted_iota(jnp.int32, (32, 128), 1) < 64
    evens, odds = [], []
    for pairing in range(H // 2):
        one = dsr[pl.ds(2 * pairing, 32, stride=HP), :]
        two = dsr[pl.ds(2 * pairing + 1, 32, stride=HP), :]
        evens.append(jnp.where(left32, one, pltpu.roll(two, 64, 1)).astype(BF16))
        odds.append(jnp.where(left32, pltpu.roll(one, 64, 1), two).astype(BF16))
    lhs = jnp.concatenate((jnp.concatenate(evens, 1), jnp.concatenate(odds, 1)), 0)
    qside = nn(lhs, kbd[...])
    for t in range(4):
        for odd in range(2):
            qres[t, pl.ds(odd, 32, stride=2), :] = qside[32 * odd : 32 * odd + 32, 128 * t : 128 * t + 128]
    row_sums = exact_nn(qres[1], expand_k)
    for t in (2, 3):
        at = 128 * (t - 2)
        qres[t] = -2.0 * ps_lane[t - 2] * (
            row_sums[:, at : at + 128] * qf[:, 128 * t : 128 * t + 128] - qres[t]
        )
    for t in (0, 1):
        qres[t] = SCALE_Q * qres[t]
    for s in range(PEERS):
        for t in range(4):
            qch[s, 4 * t : 4 * t + 4, :] = qres[t, 4 * s : 4 * s + 4, :]
    qr[c] = qch[c]
    scatter(qch, qr, "col", 6)

    wait_recv(w_row, 4)
    w_sum = w_row[0]
    for s in range(1, PEERS):
        w_sum = w_sum + w_row[s]
    w_mid[...] = w_sum
    w_col[c] = w_sum
    spread(w_mid, w_col, "col", 7)

    wb = jnp.concatenate((wb_high, wb_high, wb_low), 0)
    writes = [
        pltpu.make_async_copy(
            pair_v.at[pl.ds(1024 * n, 1024)], gpair_out.at[pl.ds(1024 * n, 1024)], out_sem.at[n]
        )
        for n in range(4)
    ]
    for n in range(4):

        @pl.loop(4 * n, 4 * n + 4)
        def _(t):
            gz = gzg[t]
            for a in range(2):
                rows = pl.ds(32 * t + 16 * a, 16)
                p = prob[rows, :]
                high = dsr[rows, :].astype(BF16)
                lhs = jnp.concatenate(
                    (
                        jnp.where(left, p, 0.0).astype(BF16),
                        jnp.where(left, 0.0, p).astype(BF16),
                        high,
                        dlo[rows, :],
                        high,
                    ),
                    0,
                )
                rhs = jnp.concatenate((gz[32 * a : 32 * a + 32], wb), 0)
                pair_v[pl.ds(256 * t + 128 * a, 128), :] = tn(lhs, rhs)

        writes[n].start()

    wait_recv(kr, 5)
    ksum = kr[0]
    for s in range(1, PEERS):
        ksum = ksum + kr[s]
    gk_out[:, 0:128] = ksum[0:4]
    gk_out[:, 128:192] = ksum[4:8, 0:64]
    gkp_out[:, 0:128] = ksum[8:12]
    gkp_out[:, 128:144] = ksum[12:16, 0:16]
    gv_out[:, 0:128] = ksum[16:20]
    gv_out[:, 128:192] = ksum[28:32, 0:64]
    gvp_out[:, 0:128] = ksum[20:24]
    gvp_out[:, 128:256] = ksum[24:28]
    gvp_out[:, 256:288] = ksum[28:32, 64:96]
    wait_recv(qr, 6)
    qsum = qr[0]
    for s in range(1, PEERS):
        qsum = qsum + qr[s]
    gq_out[:, 0:128] = qsum[0:4]
    gq_out[:, 128:192] = qsum[4:8, 0:64]
    gqp_out[:, 0:128] = qsum[8:12]
    gqp_out[:, 128:144] = qsum[12:16, 0:16]

    wait_recv(w_col, 7)
    w_sum = w_col[0]
    for s in range(1, PEERS):
        w_sum = w_sum + w_col[s]
    w_full = jnp.concatenate((w_sum, jnp.zeros((128 - HP, 128), F32)), 0)
    gbw_out[...] = jnp.transpose(w_full)[:, 0:H]

    for n, dst in enumerate((qg, kg, gzg, stat_g, w_row, kr, qr, w_col)):
        wait_send(dst, n)
    for write in writes:
        write.wait()


def on_device(
    queries, query_points, key_feats, key_points, values, value_points, pair_rep, bias_weight,
    head_weight, chain_bias, chain_ids, live_mask, cot_scalar, cot_points, cot_pair,
):
    any_spec = pl.BlockSpec(memory_space=pl.ANY)
    vmem_spec = pl.BlockSpec(memory_space=pltpu.VMEM)

    def vm(*shape, kind=F32):
        return pltpu.VMEM(shape, kind)

    scratch = [
        vm(4, 192, kind=BF16), vm(4, 144, kind=BF16), vm(4, 192, kind=BF16), vm(4, 144, kind=BF16),
        vm(4, 192, kind=BF16), vm(4, 288, kind=BF16), vm(4096, 128), vm(128, H),
        pltpu.SMEM((H,), F32), pltpu.SMEM((H,), F32),
        pltpu.SMEM((8, 128), jnp.int32), pltpu.SMEM((8, 128), jnp.int32),
        vm(8, 128, kind=jnp.int32), vm(8, 128, kind=jnp.int32),
        vm(4, 192, kind=BF16), vm(4, 288, kind=BF16), vm(4, 1536, kind=BF16),
        vm(32, 128), vm(64, 128), vm(32, 128, kind=BF16), vm(32, 128, kind=BF16), vm(64, 128, kind=BF16),
        vm(PEERS, 32, 128, kind=BF16), vm(PEERS, 32, 128, kind=BF16), vm(PEERS, 64, 128, kind=BF16),
        vm(PEERS, 32, 128),
        vm(TILE, 1024), vm(TILE, 1024), vm(2 * TILE, 1024, kind=BF16), vm(2, 512, 1024, kind=BF16),
        vm(H * TILE, 512, kind=BF16), vm(4096, 256, kind=BF16), vm(512, 128), vm(512, 128), vm(512, 128),
        vm(512, 128), vm(512, 128), vm(512, 128), vm(512, 128, kind=BF16),
        vm(3, HP, 128), vm(HP, 128), vm(PEERS, HP, 128), vm(HP, 128), vm(PEERS, HP, 128), vm(HP, 128),
        vm(PEERS, HP, 128),
        vm(TILE, 1024), vm(PEERS, 32, 128), vm(PEERS, 32, 128), vm(4, TILE, 128), vm(PEERS, 16, 128),
        vm(PEERS, 16, 128),
        pltpu.SemaphoreType.DMA((17,)), pltpu.SemaphoreType.DMA((4,)),
        pltpu.SemaphoreType.DMA((8,)), pltpu.SemaphoreType.DMA((8,)),
    ]
    out_shape = [
        jax.ShapeDtypeStruct(shape, F32)
        for shape in ((4, 192), (4, 144), (4, 192), (4, 144), (4, 192), (4, 288), (4096, 128), (128, H))
    ]
    out = pl.pallas_call(
        kernel,
        out_shape=out_shape,
        in_specs=[any_spec] * 15,
        out_specs=[vmem_spec] * 6 + [any_spec, vmem_spec],
        scratch_shapes=scratch,
        compiler_params=pltpu.CompilerParams(
            collective_id=0, has_side_effects=True, vmem_limit_bytes=40 * 2**20
        ),
        cost_estimate=pl.CostEstimate(flops=10**9, bytes_accessed=5 * 2**20, transcendentals=10**5),
    )(
        queries, query_points, key_feats, key_points, values, value_points,
        pair_rep.reshape(4096, 128), bias_weight, head_weight, chain_bias,
        chain_ids.reshape(8, 128), live_mask.reshape(8, 128), cot_scalar, cot_points, cot_pair,
    )
    return (*out[:6], out[6].reshape(TILE, TILE, 128), out[7])


def solution(mesh):
    rc, cr = P(("row", "col"), None), P(("col", "row"), None)
    tile = P("row", "col", None)
    return jax.shard_map(
        on_device,
        mesh=mesh,
        in_specs=(rc, rc, cr, cr, cr, cr, tile, P(), P(), P(), P(), P(), rc, rc, rc),
        out_specs=(rc, rc, cr, cr, cr, cr, tile, P()),
        check_vma=False,
    )
```

```python
import math

import jax
import jax.numpy as jnp
from jax import lax
from jax.experimental import pallas as pl
from jax.experimental.pallas import tpu as pltpu
from jax.sharding import PartitionSpec as P

MESH = pl.DeviceIdType.MESH
NEG_FILL = -1e30
F32 = jnp.float32
BF16 = jnp.bfloat16
H = 12
HP = 16
TILE = 64
PEERS = 16
VMEM_LIMIT = 60 * 2**20
CHUNKS = 8
W_LOGIT = math.sqrt(1.0 / 3.0)
W_POINT = math.sqrt(2.0 / 36.0)
SCALE_Q = W_LOGIT / 4.0


def nn(a, b):
    return lax.dot_general(a, b, (((1,), (0,)), ((), ())), preferred_element_type=F32)


def tn(a, b):
    return lax.dot_general(a, b, (((0,), (0,)), ((), ())), preferred_element_type=F32)


def exact_nn(a, b):
    return lax.dot_general(
        a, b, (((1,), (0,)), ((), ())), preferred_element_type=F32, precision=lax.Precision.HIGHEST
    )


def split(x):
    high = x.astype(BF16)
    return high, (x - high.astype(F32)).astype(BF16)


def head_masks(sub, lane):
    def block(col, width):
        return (col >= sub * width) & (col < sub * width + width)

    tiles = [
        block(lane, 16),
        ((lane < 64) & block(lane + 128, 16)) | (lane == sub + 64) | (lane == sub + 80),
        block(lane, 12),
        (lane < 16) & block(lane + 128, 12),
        block(lane, 16),
        block(lane, 24),
        block(lane + 128, 24),
        ((lane < 64) & block(lane + 128, 16)) | ((lane >= 64) & (lane < 96) & block(lane + 192, 24)),
    ]
    return [(tile & (sub < H)).astype(F32) for tile in tiles]


def kernel(
    q_in, qp_in, k_in, kp_in, v_in, vp_in, pair_in, bw_in, hw_in, cb_in, chain_in, live_in,
    gs_in, gp_in, gz_in,
    gq_out, gqp_out, gk_out, gkp_out, gv_out, gvp_out, gpair_out, gbw_out,
    q_v, qp_v, k_v, kp_v, v_v, vp_v, pair_v, bw_v, hw_s, cb_s, chain_s, live_s, chain_v, live_v,
    gs_v, gp_v, gz_v,
    pack, gz32, qsend, ksend, gzsend, qg, kg, gzg, blk, gz12, gz16, gzp,
    qf, kf, kdup, qbd, kbd, pp, ppt, base, qsq, expo, dprob, prob, dsr, dlo,
    stats, stat_send, stat_g, w_send, w_row, w_mid, w_col,
    kres, kch, kr, qres, qch, qr,
    gq_v, gqp_v, gk_v, gkp_v, gv_v, gvp_v, gbw_v,
    in_sem, out_sem, send_sem, recv_sem,
):
    r = lax.axis_index("row")
    c = lax.axis_index("col")
    barrier = pltpu.get_barrier_semaphore()

    def fan(axis, act):
        if axis == "col":
            y, z = c // 8, lax.rem(c, 8)

            def at(dy, j):
                dz = 4 + (1 - 2 * lax.rem(j, 2)) * ((j + 1) // 2)
                act((r, lax.rem(y + dy, 2) * 8 + lax.rem(z + dz, 8)))

            @pl.loop(0, 3)
            def _(j):
                at(1, j)

            @pl.loop(3, 8)
            def _(j):
                at(1, j)
                at(0, j - 3)

            @pl.loop(5, 7)
            def _(j):
                at(0, j)
        else:
            x, y, core = r // 4, lax.rem(r // 2, 2), lax.rem(r, 2)

            def at(dx, dy, dc):
                act((lax.rem(x + dx, 4) * 4 + lax.rem(y + dy, 2) * 2 + lax.rem(core + dc, 2), c))

            @pl.loop(0, 3)
            def _(m):
                dx = 2 + (1 - 2 * lax.rem(m, 2)) * ((m + 1) // 2)
                at(dx, 1, 1)
                at(dx, 1, 0)
                at(dx, 0, 1)
                at(dx, 0, 0)

            at(0, 1, 1)
            at(0, 1, 0)
            at(0, 0, 1)

    def greet(peer):
        pl.semaphore_signal(barrier, inc=1, device_id=peer, device_id_type=MESH)

    fan("col", greet)
    fan("row", greet)

    loads = [
        pltpu.make_async_copy(src, dst, in_sem.at[n])
        for n, (src, dst) in enumerate(
            (
                (pair_in, pair_v), (q_in, q_v), (qp_in, qp_v), (k_in, k_v), (kp_in, kp_v), (v_in, v_v),
                (vp_in, vp_v), (bw_in, bw_v), (hw_in, hw_s), (cb_in, cb_s), (chain_in, chain_s),
                (live_in, live_s), (chain_in, chain_v), (live_in, live_v), (gs_in, gs_v), (gp_in, gp_v),
                (gz_in, gz_v),
            )
        )
    ]
    for load in loads[1:]:
        load.start()
    loads[0].start()
    for load in loads[1:]:
        load.wait()

    sub = lax.broadcasted_iota(jnp.int32, (HP, 128), 0)
    lane = lax.broadcasted_iota(jnp.int32, (HP, 128), 1)
    left = lane < 64
    masks = head_masks(sub, lane)

    gz16[...] = jnp.zeros_like(gz16)

    live4 = jnp.zeros((4, 128), F32)
    sub4 = lax.broadcasted_iota(jnp.int32, (4, 128), 0)
    first = r * TILE + c * 4
    for i in range(4):
        at = first + i
        live4 = jnp.where(sub4 == i, live_s[at // 128, lax.rem(at, 128)].astype(F32), live4)

    def pack_block(scalars, points, vals, vpoints, ones, live, send):
        pack[...] = jnp.zeros_like(pack)
        a, b = scalars[...].astype(F32), points[...].astype(F32)
        d, e = vals[...].astype(F32), vpoints[...].astype(F32)
        pack[0:4, :] = a[:, 0:128]
        pack[4:8, 0:64] = a[:, 128:192]
        pack[4:8, ones : ones + 16] = jnp.ones((4, 16), F32)
        pack[8:12, :] = b[:, 0:128]
        pack[12:16, 0:16] = b[:, 128:144]
        pack[16:20, :] = d[:, 0:128] * live
        pack[20:24, :] = e[:, 0:128] * live
        pack[24:28, :] = e[:, 128:256] * live
        pack[28:32, 0:64] = d[:, 128:192] * live[:, 0:64]
        pack[28:32, 64:96] = e[:, 256:288] * live[:, 0:32]
        send[...] = pack[...].astype(BF16)

    pack_block(q_v, qp_v, gs_v, gp_v, 64, live4, qsend)
    pack_block(k_v, kp_v, v_v, vp_v, 80, jnp.ones((4, 128), F32), ksend)
    for h in range(H):
        gz32[pl.ds(h, 4, stride=H), :] = gz_v[:, 128 * h : 128 * h + 128].astype(F32) * live4
    gzsend[...] = gz32[...].astype(BF16)
    qg[c] = qsend[...]
    kg[r] = ksend[...]
    gzg[c] = gzsend[...]

    ps = jnp.zeros((HP, 128), F32)
    cb = jnp.zeros((HP, 128), F32)
    for h in range(H):
        ps = jnp.where(sub == h, hw_s[h], ps)
        cb = jnp.where(sub == h, cb_s[h], cb)
    ps = W_LOGIT * ps * W_POINT / 2.0
    ps_lane = [jnp.sum(masks[t] * ps, 0, keepdims=True) for t in (2, 3)]
    bw_t = jnp.concatenate((bw_v[...], jnp.zeros((HP - H, 128), F32)), 0)
    bw_high, bw_low = split(bw_t)
    wb_high, wb_low = split(W_LOGIT * bw_t)
    col_at = c * TILE
    chain_k = chain_v[pl.ds(col_at // 128, 1), :]
    live_k = live_v[pl.ds(col_at // 128, 1), :].astype(F32)
    half = lax.rem(c, 2)
    lane1 = lax.broadcasted_iota(jnp.int32, (1, 128), 1)
    own = (lane1 // 64) == half
    chain_k = jnp.where(own, chain_k, pltpu.roll(chain_k, 64, 1))
    live_k = jnp.where(own, live_k, pltpu.roll(live_k, 64, 1))

    loads[0].wait()
    bias_lhs = jnp.concatenate(
        (jnp.concatenate((bw_high, bw_high), 1), jnp.concatenate((bw_low, bw_low), 1)), 0
    )

    @pl.loop(0, 16)
    def _(t):
        high, low = split(pair_v[pl.ds(256 * t, 256), :])
        both = jnp.concatenate((high, low), 1)
        pp[pl.ds(256 * t, 256), :] = both
        both_t = jnp.transpose(both)
        ppt[t] = both_t
        res = nn(bias_lhs, both_t)
        res = res[0:HP] + res[HP : 2 * HP]
        for a in range(2):
            at = r * TILE + 4 * t + 2 * a
            chain_q = jnp.where(
                lane1 < 64, chain_s[at // 128, lax.rem(at, 128)], chain_s[(at + 1) // 128, lax.rem(at + 1, 128)]
            )
            same = (chain_q == chain_k).astype(F32)
            base[pl.ds(32 * t + 16 * a, 16), :] = W_LOGIT * (res[:, 128 * a : 128 * a + 128] + cb * same)

    pl.semaphore_wait(barrier, 2 * (PEERS - 1))

    def spread(src, dst, axis, n):
        me = c if axis == "col" else r

        def act(peer):
            pltpu.make_async_remote_copy(
                src_ref=src,
                dst_ref=dst.at[me],
                send_sem=send_sem.at[n],
                recv_sem=recv_sem.at[n],
                device_id=peer,
                device_id_type=MESH,
            ).start()

        fan(axis, act)

    def scatter(src, dst, axis, n):
        me = c if axis == "col" else r

        def act(peer):
            pltpu.make_async_remote_copy(
                src_ref=src.at[peer[1] if axis == "col" else peer[0]],
                dst_ref=dst.at[me],
                send_sem=send_sem.at[n],
                recv_sem=recv_sem.at[n],
                device_id=peer,
                device_id_type=MESH,
            ).start()

        fan(axis, act)

    def wait_recv(dst, n):
        part = dst.at[pl.ds(0, PEERS - 1)]
        pltpu.make_async_copy(part, part, recv_sem.at[n]).wait()

    def wait_send(dst, n):
        part = dst.at[pl.ds(0, PEERS - 1)]
        pltpu.make_async_copy(part, part, send_sem.at[n]).wait()

    spread(qsend, qg, "col", 0)
    spread(ksend, kg, "row", 1)
    spread(gzsend, gzg, "col", 2)

    def assemble(got, full):
        blk[...] = got[...].astype(F32)
        for s in range(PEERS):
            for t in range(8):
                full[4 * s : 4 * s + 4, 128 * t : 128 * t + 128] = blk[s, 4 * t : 4 * t + 4, :]

    wait_recv(kg, 1)
    assemble(kg, kf)
    k_t = jnp.transpose(kf[...])
    k_t = jnp.concatenate((k_t, k_t), 1)
    kdup[...] = k_t.astype(BF16)
    for h in range(H):
        for t in range(4):
            kbd[TILE * h : TILE * h + TILE, 128 * t : 128 * t + 128] = (
                kf[:, 128 * t : 128 * t + 128] * masks[t][h : h + 1, :]
            ).astype(BF16)
    point_mask = jnp.concatenate((masks[2], masks[3]), 1)
    point_mask16 = point_mask.astype(BF16)
    square_high, square_low = split(k_t[256:512] * k_t[256:512])
    k_sq = nn(point_mask16, square_high) + nn(point_mask16, square_low)

    wait_recv(qg, 0)
    assemble(qg, qf)

    @pl.loop(0, 8, unroll=8)
    def _(b):
        eight = qf[pl.ds(pl.multiple_of(8 * b, 8), 8), :]
        for p in range(4):
            rows = pl.ds(64 * b + HP * p, HP)
            sums = []
            for odd in range(2):
                square = jnp.zeros((HP, 128), F32)
                for t in range(8):
                    value = eight[2 * p + odd : 2 * p + odd + 1, 128 * t : 128 * t + 128] * masks[t]
                    qbd[odd, rows, 128 * t : 128 * t + 128] = value.astype(BF16)
                    if t in (2, 3):
                        square = square + value * value
                sums.append(jnp.sum(square, 1, keepdims=True))
            qsq[rows, :] = jnp.where(left, sums[0], sums[1])

    half_of = lax.broadcasted_iota(jnp.int32, (256, 128), 0) % 128 // 64
    parity = lax.broadcasted_iota(jnp.int32, (256, 128), 1) % 2
    half_ones = (half_of == parity).astype(F32).astype(BF16)

    def half_sums(x):
        return nn(jnp.concatenate(split(x), 1), half_ones)

    lane_pair = lane // 2
    stats[...] = jnp.zeros_like(stats)
    lane3 = lax.broadcasted_iota(jnp.int32, (8, HP, 128), 2)
    left3 = lane3 < 64

    @pl.loop(0, 4, unroll=4)
    def _(b):
        rows = pl.ds(128 * b, 128)
        parts = []
        for k0, k1 in ((0, 256), (256, 512), (512, 1024)):
            both = nn(jnp.concatenate((qbd[0, rows, k0:k1], qbd[1, rows, k0:k1]), 0), kdup[k0:k1, :])
            both = both.reshape(2, 8, HP, 128)
            parts.append(jnp.where(left3, both[0], both[1]))
        dprob[rows, :] = parts[2].reshape(128, 128)
        distance = qsq[rows, :].reshape(8, HP, 128) + k_sq - 2.0 * parts[1]
        logits = base[rows, :].reshape(8, HP, 128) + SCALE_Q * parts[0] - ps * distance
        logits = jnp.where(live_k > 0, logits, NEG_FILL)
        max0 = jnp.max(jnp.where(left3, logits, NEG_FILL), 2, keepdims=True)
        max1 = jnp.max(jnp.where(left3, NEG_FILL, logits), 2, keepdims=True)
        e = jnp.exp(logits - jnp.where(left3, max0, max1)) * live_k
        e = e.reshape(128, 128)
        expo[rows, :] = e
        sums = half_sums(e)
        acc_m, acc_s = stats[0], stats[1]
        for i in range(8):
            at = 16 * b + 2 * i
            acc_m = jnp.where(lane == at, max0[i], jnp.where(lane == at + 1, max1[i], acc_m))
            acc_s = jnp.where(lane_pair == 8 * b + i, sums[HP * i : HP * i + HP], acc_s)
        stats[0] = acc_m
        stats[1] = acc_s

    wait_recv(gzg, 2)

    gz12[...] = gzg[...].astype(F32).reshape(PEERS * 4 * H, 128)

    @pl.loop(0, PEERS, unroll=PEERS)
    def _(t):
        for i in range(4):
            gz16[pl.ds(64 * t + HP * i, H), :] = gz12[pl.ds(48 * t + H * i, H), :]

    gzp[...] = gz16[...].astype(BF16).reshape(PEERS, 4 * HP, 128)

    @pl.loop(0, 16, unroll=16)
    def _(t):
        gz = gzp[t]
        res = nn(jnp.concatenate((gz, gz), 1), ppt[t])
        for a in range(2):
            rows = pl.ds(32 * t + 16 * a, 16)
            tile = res[32 * a : 32 * a + 32, 128 * a : 128 * a + 128]
            dprob[rows, :] = dprob[rows, :] + jnp.where(left, tile[0:16], tile[16:32])

    sums = half_sums(expo[...] * dprob[...])
    acc = jnp.zeros((HP, 128), F32)
    for p in range(32):
        acc = jnp.where(lane_pair == p, sums[HP * p : HP * p + HP], acc)
    stats[2] = acc

    row_max, row_sum = stats[0], stats[1]
    any_live = row_sum > 0
    safe = jnp.where(any_live, row_sum, 1.0)
    lse = jnp.where(any_live, row_max + jnp.log(safe), NEG_FILL)
    mean = jnp.where(any_live, stats[2] / safe, 0.0)
    stat_send[...] = jnp.where(left, lse, pltpu.roll(mean, 64, 1))
    stat_g[c] = stat_send[...]
    spread(stat_send, stat_g, "col", 3)
    wait_recv(stat_g, 3)
    top = stat_g[0]
    for s in range(1, PEERS):
        top = jnp.maximum(top, stat_g[s])
    total = jnp.zeros((HP, 128), F32)
    dsum = jnp.zeros((HP, 128), F32)
    for s in range(PEERS):
        got = stat_g[s]
        weight = jnp.exp(got - top)
        total = total + weight
        dsum = dsum + weight * pltpu.roll(got, 64, 1)
    stats[0] = jnp.exp(row_max - top) / total
    stats[1] = dsum / total

    @pl.loop(0, 8, unroll=8)
    def _(b):
        scale = pltpu.roll(stats[0], lax.rem(128 - 8 * b, 128), 1)
        mean_all = pltpu.roll(stats[1], lax.rem(128 - 8 * b, 128), 1)
        for i in range(4):
            rows = pl.ds(64 * b + 16 * i, 16)
            factor = jnp.where(left, scale[:, 2 * i : 2 * i + 1], scale[:, 2 * i + 1 : 2 * i + 2])
            shift = jnp.where(left, mean_all[:, 2 * i : 2 * i + 1], mean_all[:, 2 * i + 1 : 2 * i + 2])
            p = expo[rows, :] * factor
            ds = p * (dprob[rows, :] - shift)
            high, low = split(ds)
            prob[rows, :] = p.astype(BF16).astype(F32)
            dsr[rows, :] = high.astype(F32)
            dlo[rows, :] = low

    def weight_step(t, acc):
        high = dsr[pl.ds(32 * t, 32), :].astype(BF16)
        low = dlo[pl.ds(32 * t, 32), :]
        lhs = jnp.concatenate(
            (
                jnp.concatenate((high[0:16], high[16:32]), 1),
                jnp.concatenate((low[0:16], low[16:32]), 1),
            ),
            0,
        )
        return acc + nn(lhs, pp[pl.ds(256 * t, 256), :])

    w_all = lax.fori_loop(0, 16, weight_step, jnp.zeros((2 * HP, 256), F32), unroll=16)
    w_all = w_all[:, 0:128] + w_all[:, 128:256]
    w_send[...] = W_LOGIT * (w_all[0:HP] + w_all[HP : 2 * HP])
    w_row[r] = w_send[...]
    spread(w_send, w_row, "row", 4)

    ds_t = jnp.transpose(dsr[...]).astype(BF16)
    prob_t = jnp.transpose(prob[...]).astype(BF16)
    kside = nn(ds_t[0:TILE], qbd[0, :, 0:512]) + nn(ds_t[TILE : 2 * TILE], qbd[1, :, 0:512])
    vside = nn(prob_t[0:TILE], qbd[0, :, 512:1024]) + nn(prob_t[TILE : 2 * TILE], qbd[1, :, 512:1024])
    expand_q = jnp.concatenate((jnp.zeros((64, 256), F32), point_mask, jnp.zeros((48, 256), F32)), 0)
    expand_k = jnp.concatenate((jnp.zeros((80, 256), F32), point_mask, jnp.zeros((32, 256), F32)), 0)
    ps_row = jnp.concatenate(ps_lane, 1)
    kres[:, 0:256] = SCALE_Q * kside[:, 0:256]
    kres[:, 256:512] = -2.0 * ps_row * (
        exact_nn(kside[:, 128:256], expand_q) * kf[:, 256:512] - kside[:, 256:512]
    )
    kres[:, 512:1024] = vside
    for s in range(PEERS):
        for t in range(8):
            kch[s, 4 * t : 4 * t + 4, :] = kres[4 * s : 4 * s + 4, 128 * t : 128 * t + 128]
    kr[r] = kch[r]
    scatter(kch, kr, "row", 5)

    left32 = lax.broadcasted_iota(jnp.int32, (32, 128), 1) < 64
    evens, odds = [], []
    for pairing in range(H // 2):
        one = dsr[pl.ds(2 * pairing, 32, stride=HP), :]
        two = dsr[pl.ds(2 * pairing + 1, 32, stride=HP), :]
        evens.append(jnp.where(left32, one, pltpu.roll(two, 64, 1)).astype(BF16))
        odds.append(jnp.where(left32, pltpu.roll(one, 64, 1), two).astype(BF16))
    lhs = jnp.concatenate((jnp.concatenate(evens, 1), jnp.concatenate(odds, 1)), 0)
    qside = nn(lhs, kbd[...])
    for t in range(4):
        for odd in range(2):
            qres[t, pl.ds(odd, 32, stride=2), :] = qside[32 * odd : 32 * odd + 32, 128 * t : 128 * t + 128]
    row_sums = exact_nn(qres[1], expand_k)
    for t in (2, 3):
        at = 128 * (t - 2)
        qres[t] = -2.0 * ps_lane[t - 2] * (
            row_sums[:, at : at + 128] * qf[:, 128 * t : 128 * t + 128] - qres[t]
        )
    for t in (0, 1):
        qres[t] = SCALE_Q * qres[t]
    for s in range(PEERS):
        for t in range(4):
            qch[s, 4 * t : 4 * t + 4, :] = qres[t, 4 * s : 4 * s + 4, :]
    qr[c] = qch[c]
    scatter(qch, qr, "col", 6)

    wait_recv(w_row, 4)
    w_sum = w_row[0]
    for s in range(1, PEERS):
        w_sum = w_sum + w_row[s]
    w_mid[...] = w_sum
    w_col[c] = w_sum
    spread(w_mid, w_col, "col", 7)

    wb = jnp.concatenate((wb_high, wb_high, wb_low), 0)
    writes = [
        pltpu.make_async_copy(
            pair_v.at[pl.ds(1024 * n, 1024)], gpair_out.at[pl.ds(1024 * n, 1024)], out_sem.at[n]
        )
        for n in range(4)
    ]
    for n in range(4):

        @pl.loop(4 * n, 4 * n + 4, unroll=4)
        def _(t):
            gz = gzp[t]
            for a in range(2):
                rows = pl.ds(32 * t + 16 * a, 16)
                p = prob[rows, :]
                high = dsr[rows, :].astype(BF16)
                lhs = jnp.concatenate(
                    (
                        jnp.where(left, p, 0.0).astype(BF16),
                        jnp.where(left, 0.0, p).astype(BF16),
                        high,
                        dlo[rows, :],
                        high,
                    ),
                    0,
                )
                rhs = jnp.concatenate((gz[32 * a : 32 * a + 32], wb), 0)
                pair_v[pl.ds(256 * t + 128 * a, 128), :] = tn(lhs, rhs)

        writes[n].start()

    small = [
        pltpu.make_async_copy(src, dst, out_sem.at[4 + n])
        for n, (src, dst) in enumerate(
            (
                (gq_v, gq_out), (gqp_v, gqp_out), (gk_v, gk_out), (gkp_v, gkp_out), (gv_v, gv_out),
                (gvp_v, gvp_out), (gbw_v, gbw_out),
            )
        )
    ]
    wait_recv(kr, 5)
    ksum = kr[0]
    for s in range(1, PEERS):
        ksum = ksum + kr[s]
    gk_v[:, 0:128] = ksum[0:4]
    gk_v[:, 128:192] = ksum[4:8, 0:64]
    gkp_v[:, 0:128] = ksum[8:12]
    gkp_v[:, 128:144] = ksum[12:16, 0:16]
    gv_v[:, 0:128] = ksum[16:20]
    gv_v[:, 128:192] = ksum[28:32, 0:64]
    gvp_v[:, 0:128] = ksum[20:24]
    gvp_v[:, 128:256] = ksum[24:28]
    gvp_v[:, 256:288] = ksum[28:32, 64:96]
    for n in range(2, 6):
        small[n].start()
    wait_recv(qr, 6)
    qsum = qr[0]
    for s in range(1, PEERS):
        qsum = qsum + qr[s]
    gq_v[:, 0:128] = qsum[0:4]
    gq_v[:, 128:192] = qsum[4:8, 0:64]
    gqp_v[:, 0:128] = qsum[8:12]
    gqp_v[:, 128:144] = qsum[12:16, 0:16]

    small[0].start()
    small[1].start()

    wait_recv(w_col, 7)
    w_sum = w_col[0]
    for s in range(1, PEERS):
        w_sum = w_sum + w_col[s]
    gbw_v[...] = w_sum[0:H]
    small[6].start()

    for n, dst in enumerate((qg, kg, gzg, stat_g, w_row, kr, qr, w_col)):
        wait_send(dst, n)
    for write in writes + small:
        write.wait()


def finish(*refs):
    srcs, dsts, held, sem = refs[0:8], refs[8:16], refs[16:24], refs[24]
    rows = 4096 // CHUNKS
    parts = [(n, None) for n in range(8) if n != 6] + [(6, pl.ds(rows * k, rows)) for k in range(CHUNKS)]
    moves = []
    for at, (n, part) in enumerate(parts):
        src, mid, dst = srcs[n], held[n], dsts[n]
        if part is not None:
            src, mid, dst = src.at[part], mid.at[part], dst.at[part]
        moves.append(
            (pltpu.make_async_copy(src, mid, sem.at[0, at]), pltpu.make_async_copy(mid, dst, sem.at[1, at]))
        )
    for load, _ in moves:
        load.start()
    for load, store in moves:
        load.wait()
        store.start()
    for _, store in moves:
        store.wait()


def on_device(
    queries, query_points, key_feats, key_points, values, value_points, pair_rep, bias_weight,
    head_weight, chain_bias, chain_ids, live_mask, cot_scalar, cot_points, cot_pair,
):
    any_spec = pl.BlockSpec(memory_space=pl.ANY)

    def vm(*shape, kind=F32):
        return pltpu.VMEM(shape, kind)

    scratch = [
        vm(4, 192, kind=BF16), vm(4, 144, kind=BF16), vm(4, 192, kind=BF16), vm(4, 144, kind=BF16),
        vm(4, 192, kind=BF16), vm(4, 288, kind=BF16), vm(4096, 128), vm(H, 128),
        pltpu.SMEM((H,), F32), pltpu.SMEM((H,), F32),
        pltpu.SMEM((8, 128), jnp.int32), pltpu.SMEM((8, 128), jnp.int32),
        vm(8, 128, kind=jnp.int32), vm(8, 128, kind=jnp.int32),
        vm(4, 192, kind=BF16), vm(4, 288, kind=BF16), vm(4, 1536, kind=BF16),
        vm(32, 128), vm(4 * H, 128), vm(32, 128, kind=BF16), vm(32, 128, kind=BF16), vm(4 * H, 128, kind=BF16),
        vm(PEERS, 32, 128, kind=BF16), vm(PEERS, 32, 128, kind=BF16), vm(PEERS, 4 * H, 128, kind=BF16),
        vm(PEERS, 32, 128), vm(PEERS * 4 * H, 128), vm(PEERS * 4 * HP, 128), vm(PEERS, 4 * HP, 128, kind=BF16),
        vm(TILE, 1024), vm(TILE, 1024), vm(1024, 128, kind=BF16), vm(2, 512, 1024, kind=BF16),
        vm(H * TILE, 512, kind=BF16), vm(4096, 256, kind=BF16), vm(16, 256, 256, kind=BF16), vm(512, 128), vm(512, 128), vm(512, 128),
        vm(512, 128), vm(512, 128), vm(512, 128), vm(512, 128, kind=BF16),
        vm(3, HP, 128), vm(HP, 128), vm(PEERS, HP, 128), vm(HP, 128), vm(PEERS, HP, 128), vm(HP, 128),
        vm(PEERS, HP, 128),
        vm(TILE, 1024), vm(PEERS, 32, 128), vm(PEERS, 32, 128), vm(4, TILE, 128), vm(PEERS, 16, 128),
        vm(PEERS, 16, 128),
        vm(4, 192), vm(4, 144), vm(4, 192), vm(4, 144), vm(4, 192), vm(4, 288), vm(H, 128),
        pltpu.SemaphoreType.DMA((17,)), pltpu.SemaphoreType.DMA((11,)),
        pltpu.SemaphoreType.DMA((8,)), pltpu.SemaphoreType.DMA((8,)),
    ]
    out_shape = [
        jax.ShapeDtypeStruct(shape, F32)
        for shape in ((4, 192), (4, 144), (4, 192), (4, 144), (4, 192), (4, 288), (4096, 128), (H, 128))
    ]
    out = pl.pallas_call(
        kernel,
        out_shape=out_shape,
        in_specs=[any_spec] * 15,
        out_specs=[any_spec] * 8,
        scratch_shapes=scratch,
        compiler_params=pltpu.CompilerParams(
            collective_id=0, has_side_effects=True, vmem_limit_bytes=VMEM_LIMIT
        ),
        cost_estimate=pl.CostEstimate(flops=10**9, bytes_accessed=5 * 2**20, transcendentals=10**5),
    )(
        queries, query_points, key_feats, key_points, values, value_points,
        pair_rep.reshape(4096, 128), bias_weight.T, head_weight, chain_bias,
        chain_ids.reshape(8, 128), live_mask.reshape(8, 128), cot_scalar, cot_points, cot_pair,
    )
    out = pl.pallas_call(
        finish,
        out_shape=out_shape,
        in_specs=[any_spec] * 8,
        out_specs=[any_spec] * 8,
        scratch_shapes=[vm(*shape.shape) for shape in out_shape] + [pltpu.SemaphoreType.DMA((2, 7 + CHUNKS))],
        compiler_params=pltpu.CompilerParams(vmem_limit_bytes=VMEM_LIMIT),
    )(*out)
    return (*out[:6], out[6].reshape(TILE, TILE, 128), out[7].T)


def solution(mesh):
    rc, cr = P(("row", "col"), None), P(("col", "row"), None)
    tile = P("row", "col", None)
    return jax.shard_map(
        on_device,
        mesh=mesh,
        in_specs=(rc, rc, cr, cr, cr, cr, tile, P(), P(), P(), P(), P(), rc, rc, rc),
        out_specs=(rc, rc, cr, cr, cr, cr, tile, P()),
        check_vma=False,
    )
```

```python
import math

import jax
import jax.numpy as jnp
from jax import lax
from jax.experimental import pallas as pl
from jax.experimental.pallas import tpu as pltpu
from jax.sharding import PartitionSpec as P

MESH = pl.DeviceIdType.MESH
NEG_FILL = -1e30
F32 = jnp.float32
BF16 = jnp.bfloat16
H = 12
HP = 16
TILE = 64
PEERS = 16
VMEM_LIMIT = 40 * 2**20
W_LOGIT = math.sqrt(1.0 / 3.0)
W_POINT = math.sqrt(2.0 / 36.0)
SCALE_Q = W_LOGIT / 4.0


def nn(a, b):
    return lax.dot_general(a, b, (((1,), (0,)), ((), ())), preferred_element_type=F32)


def tn(a, b):
    return lax.dot_general(a, b, (((0,), (0,)), ((), ())), preferred_element_type=F32)


def exact_nn(a, b):
    return lax.dot_general(
        a, b, (((1,), (0,)), ((), ())), preferred_element_type=F32, precision=lax.Precision.HIGHEST
    )


def split(x):
    high = x.astype(BF16)
    return high, (x - high.astype(F32)).astype(BF16)


def head_masks(sub, lane):
    def block(col, width):
        return (col >= sub * width) & (col < sub * width + width)

    tiles = [
        block(lane, 16),
        ((lane < 64) & block(lane + 128, 16)) | (lane == sub + 64) | (lane == sub + 80),
        block(lane, 12),
        (lane < 16) & block(lane + 128, 12),
        block(lane, 16),
        block(lane, 24),
        block(lane + 128, 24),
        ((lane < 64) & block(lane + 128, 16)) | ((lane >= 64) & (lane < 96) & block(lane + 192, 24)),
    ]
    return [(tile & (sub < H)).astype(F32) for tile in tiles]


def kernel(
    q_in, qp_in, k_in, kp_in, v_in, vp_in, pair_in, bw_in, hw_in, cb_in, chain_in, live_in,
    gs_in, gp_in, gz_in,
    gq_out, gqp_out, gk_out, gkp_out, gv_out, gvp_out, gpair_out, gbw_out,
    q_v, qp_v, k_v, kp_v, v_v, vp_v, pair_v, bw_v, hw_s, cb_s, chain_s, live_s, chain_v, live_v,
    gs_v, gp_v, gz_v,
    pack, gz32, qsend, ksend, gzsend, qg, kg, gzg, blk, gz12, gz16, gzp,
    qf, kf, kdup, qbd, kbd, pp, ppt, base, qsq, expo, dprob, prob, dsr, dlo,
    stats, stat_send, stat_g, w_send, w_row, w_mid, w_col,
    kres, kch, kr, qres, qch, qr,
    in_sem, send_sem, recv_sem,
):
    r = lax.axis_index("row")
    c = lax.axis_index("col")
    barrier = pltpu.get_barrier_semaphore()

    def fan(axis, act):
        if axis == "col":
            y, z = c // 8, lax.rem(c, 8)

            def at(dy, j):
                dz = 4 + (1 - 2 * lax.rem(j, 2)) * ((j + 1) // 2)
                act((r, lax.rem(y + dy, 2) * 8 + lax.rem(z + dz, 8)))

            @pl.loop(0, 3)
            def _(j):
                at(1, j)

            @pl.loop(3, 8)
            def _(j):
                at(1, j)
                at(0, j - 3)

            @pl.loop(5, 7)
            def _(j):
                at(0, j)
        else:
            x, y, core = r // 4, lax.rem(r // 2, 2), lax.rem(r, 2)

            def at(dx, dy, dc):
                act((lax.rem(x + dx, 4) * 4 + lax.rem(y + dy, 2) * 2 + lax.rem(core + dc, 2), c))

            @pl.loop(0, 3)
            def _(m):
                dx = 2 + (1 - 2 * lax.rem(m, 2)) * ((m + 1) // 2)
                at(dx, 1, 1)
                at(dx, 1, 0)
                at(dx, 0, 1)
                at(dx, 0, 0)

            at(0, 1, 1)
            at(0, 1, 0)
            at(0, 0, 1)

    def greet(peer):
        pl.semaphore_signal(barrier, inc=1, device_id=peer, device_id_type=MESH)

    fan("col", greet)
    fan("row", greet)

    loads = [
        pltpu.make_async_copy(src, dst, in_sem.at[n])
        for n, (src, dst) in enumerate(
            (
                (pair_in, pair_v), (q_in, q_v), (qp_in, qp_v), (k_in, k_v), (kp_in, kp_v), (v_in, v_v),
                (vp_in, vp_v), (bw_in, bw_v), (hw_in, hw_s), (cb_in, cb_s), (chain_in, chain_s),
                (live_in, live_s), (chain_in, chain_v), (live_in, live_v), (gs_in, gs_v), (gp_in, gp_v),
                (gz_in, gz_v),
            )
        )
    ]
    for load in loads[1:]:
        load.start()
    loads[0].start()
    for load in loads[1:]:
        load.wait()

    sub = lax.broadcasted_iota(jnp.int32, (HP, 128), 0)
    lane = lax.broadcasted_iota(jnp.int32, (HP, 128), 1)
    left = lane < 64
    masks = head_masks(sub, lane)

    gz16[...] = jnp.zeros_like(gz16)

    live4 = jnp.zeros((4, 128), F32)
    sub4 = lax.broadcasted_iota(jnp.int32, (4, 128), 0)
    first = r * TILE + c * 4
    for i in range(4):
        at = first + i
        live4 = jnp.where(sub4 == i, live_s[at // 128, lax.rem(at, 128)].astype(F32), live4)

    def pack_block(scalars, points, vals, vpoints, ones, live, send):
        pack[...] = jnp.zeros_like(pack)
        a, b = scalars[...].astype(F32), points[...].astype(F32)
        d, e = vals[...].astype(F32), vpoints[...].astype(F32)
        pack[0:4, :] = a[:, 0:128]
        pack[4:8, 0:64] = a[:, 128:192]
        pack[4:8, ones : ones + 16] = jnp.ones((4, 16), F32)
        pack[8:12, :] = b[:, 0:128]
        pack[12:16, 0:16] = b[:, 128:144]
        pack[16:20, :] = d[:, 0:128] * live
        pack[20:24, :] = e[:, 0:128] * live
        pack[24:28, :] = e[:, 128:256] * live
        pack[28:32, 0:64] = d[:, 128:192] * live[:, 0:64]
        pack[28:32, 64:96] = e[:, 256:288] * live[:, 0:32]
        send[...] = pack[...].astype(BF16)

    pack_block(q_v, qp_v, gs_v, gp_v, 64, live4, qsend)
    pack_block(k_v, kp_v, v_v, vp_v, 80, jnp.ones((4, 128), F32), ksend)
    for h in range(H):
        gz32[pl.ds(h, 4, stride=H), :] = gz_v[:, 128 * h : 128 * h + 128].astype(F32) * live4
    gzsend[...] = gz32[...].astype(BF16)
    qg[c] = qsend[...]
    kg[r] = ksend[...]
    gzg[c] = gzsend[...]

    ps = jnp.zeros((HP, 128), F32)
    cb = jnp.zeros((HP, 128), F32)
    for h in range(H):
        ps = jnp.where(sub == h, hw_s[h], ps)
        cb = jnp.where(sub == h, cb_s[h], cb)
    ps = W_LOGIT * ps * W_POINT / 2.0
    ps_lane = [jnp.sum(masks[t] * ps, 0, keepdims=True) for t in (2, 3)]
    bw_t = jnp.concatenate((bw_v[...], jnp.zeros((HP - H, 128), F32)), 0)
    bw_high, bw_low = split(bw_t)
    wb_high, wb_low = split(W_LOGIT * bw_t)
    col_at = c * TILE
    chain_k = chain_v[pl.ds(col_at // 128, 1), :]
    live_k = live_v[pl.ds(col_at // 128, 1), :].astype(F32)
    half = lax.rem(c, 2)
    lane1 = lax.broadcasted_iota(jnp.int32, (1, 128), 1)
    own = (lane1 // 64) == half
    chain_k = jnp.where(own, chain_k, pltpu.roll(chain_k, 64, 1))
    live_k = jnp.where(own, live_k, pltpu.roll(live_k, 64, 1))

    pl.semaphore_wait(barrier, 2 * (PEERS - 1))

    def spread(src, dst, axis, n):
        me = c if axis == "col" else r

        def act(peer):
            pltpu.make_async_remote_copy(
                src_ref=src,
                dst_ref=dst.at[me],
                send_sem=send_sem.at[n],
                recv_sem=recv_sem.at[n],
                device_id=peer,
                device_id_type=MESH,
            ).start()

        fan(axis, act)

    def scatter(src, dst, axis, n):
        me = c if axis == "col" else r

        def act(peer):
            pltpu.make_async_remote_copy(
                src_ref=src.at[peer[1] if axis == "col" else peer[0]],
                dst_ref=dst.at[me],
                send_sem=send_sem.at[n],
                recv_sem=recv_sem.at[n],
                device_id=peer,
                device_id_type=MESH,
            ).start()

        fan(axis, act)

    def wait_recv(dst, n):
        part = dst.at[pl.ds(0, PEERS - 1)]
        pltpu.make_async_copy(part, part, recv_sem.at[n]).wait()

    def wait_send(dst, n):
        part = dst.at[pl.ds(0, PEERS - 1)]
        pltpu.make_async_copy(part, part, send_sem.at[n]).wait()

    spread(qsend, qg, "col", 0)
    spread(ksend, kg, "row", 1)
    spread(gzsend, gzg, "col", 2)

    loads[0].wait()
    bias_lhs = jnp.concatenate(
        (jnp.concatenate((bw_high, bw_high), 1), jnp.concatenate((bw_low, bw_low), 1)), 0
    )

    @pl.loop(0, 16)
    def _(t):
        high, low = split(pair_v[pl.ds(256 * t, 256), :])
        both = jnp.concatenate((high, low), 1)
        pp[pl.ds(256 * t, 256), :] = both
        both_t = jnp.transpose(both)
        ppt[t] = both_t
        res = nn(bias_lhs, both_t)
        res = res[0:HP] + res[HP : 2 * HP]
        for a in range(2):
            at = r * TILE + 4 * t + 2 * a
            chain_q = jnp.where(
                lane1 < 64, chain_s[at // 128, lax.rem(at, 128)], chain_s[(at + 1) // 128, lax.rem(at + 1, 128)]
            )
            same = (chain_q == chain_k).astype(F32)
            base[pl.ds(32 * t + 16 * a, 16), :] = W_LOGIT * (res[:, 128 * a : 128 * a + 128] + cb * same)

    def assemble(got, full):
        blk[...] = got[...].astype(F32)
        for s in range(PEERS):
            for t in range(8):
                full[4 * s : 4 * s + 4, 128 * t : 128 * t + 128] = blk[s, 4 * t : 4 * t + 4, :]

    wait_recv(kg, 1)
    assemble(kg, kf)
    k_t = jnp.transpose(kf[...])
    k_t = jnp.concatenate((k_t, k_t), 1)
    kdup[...] = k_t.astype(BF16)
    for h in range(H):
        for t in range(4):
            kbd[TILE * h : TILE * h + TILE, 128 * t : 128 * t + 128] = (
                kf[:, 128 * t : 128 * t + 128] * masks[t][h : h + 1, :]
            ).astype(BF16)
    point_mask = jnp.concatenate((masks[2], masks[3]), 1)
    point_mask16 = point_mask.astype(BF16)
    square_high, square_low = split(k_t[256:512] * k_t[256:512])
    k_sq = nn(point_mask16, square_high) + nn(point_mask16, square_low)

    wait_recv(qg, 0)
    assemble(qg, qf)

    @pl.loop(0, 8, unroll=8)
    def _(b):
        eight = qf[pl.ds(pl.multiple_of(8 * b, 8), 8), :]
        for p in range(4):
            rows = pl.ds(64 * b + HP * p, HP)
            sums = []
            for odd in range(2):
                square = jnp.zeros((HP, 128), F32)
                for t in range(8):
                    value = eight[2 * p + odd : 2 * p + odd + 1, 128 * t : 128 * t + 128] * masks[t]
                    qbd[odd, rows, 128 * t : 128 * t + 128] = value.astype(BF16)
                    if t in (2, 3):
                        square = square + value * value
                sums.append(jnp.sum(square, 1, keepdims=True))
            qsq[rows, :] = jnp.where(left, sums[0], sums[1])

    half_of = lax.broadcasted_iota(jnp.int32, (256, 128), 0) % 128 // 64
    parity = lax.broadcasted_iota(jnp.int32, (256, 128), 1) % 2
    half_ones = (half_of == parity).astype(F32).astype(BF16)

    def half_sums(x):
        return nn(jnp.concatenate(split(x), 1), half_ones)

    lane_pair = lane // 2
    stats[...] = jnp.zeros_like(stats)
    lane3 = lax.broadcasted_iota(jnp.int32, (8, HP, 128), 2)
    left3 = lane3 < 64

    @pl.loop(0, 4, unroll=4)
    def _(b):
        rows = pl.ds(128 * b, 128)
        parts = []
        for k0, k1 in ((0, 256), (256, 512), (512, 1024)):
            both = nn(jnp.concatenate((qbd[0, rows, k0:k1], qbd[1, rows, k0:k1]), 0), kdup[k0:k1, :])
            both = both.reshape(2, 8, HP, 128)
            parts.append(jnp.where(left3, both[0], both[1]))
        dprob[rows, :] = parts[2].reshape(128, 128)
        distance = qsq[rows, :].reshape(8, HP, 128) + k_sq - 2.0 * parts[1]
        logits = base[rows, :].reshape(8, HP, 128) + SCALE_Q * parts[0] - ps * distance
        logits = jnp.where(live_k > 0, logits, NEG_FILL)
        max0 = jnp.max(jnp.where(left3, logits, NEG_FILL), 2, keepdims=True)
        max1 = jnp.max(jnp.where(left3, NEG_FILL, logits), 2, keepdims=True)
        e = jnp.exp(logits - jnp.where(left3, max0, max1)) * live_k
        e = e.reshape(128, 128)
        expo[rows, :] = e
        sums = half_sums(e)
        acc_m, acc_s = stats[0], stats[1]
        for i in range(8):
            at = 16 * b + 2 * i
            acc_m = jnp.where(lane == at, max0[i], jnp.where(lane == at + 1, max1[i], acc_m))
            acc_s = jnp.where(lane_pair == 8 * b + i, sums[HP * i : HP * i + HP], acc_s)
        stats[0] = acc_m
        stats[1] = acc_s

    wait_recv(gzg, 2)

    gz12[...] = gzg[...].astype(F32).reshape(PEERS * 4 * H, 128)

    @pl.loop(0, PEERS, unroll=PEERS)
    def _(t):
        for i in range(4):
            gz16[pl.ds(64 * t + HP * i, H), :] = gz12[pl.ds(48 * t + H * i, H), :]

    gzp[...] = gz16[...].astype(BF16).reshape(PEERS, 4 * HP, 128)

    @pl.loop(0, 16, unroll=16)
    def _(t):
        gz = gzp[t]
        res = nn(jnp.concatenate((gz, gz), 1), ppt[t])
        for a in range(2):
            rows = pl.ds(32 * t + 16 * a, 16)
            tile = res[32 * a : 32 * a + 32, 128 * a : 128 * a + 128]
            dprob[rows, :] = dprob[rows, :] + jnp.where(left, tile[0:16], tile[16:32])

    sums = half_sums(expo[...] * dprob[...])
    acc = jnp.zeros((HP, 128), F32)
    for p in range(32):
        acc = jnp.where(lane_pair == p, sums[HP * p : HP * p + HP], acc)
    stats[2] = acc

    row_max, row_sum = stats[0], stats[1]
    any_live = row_sum > 0
    safe = jnp.where(any_live, row_sum, 1.0)
    lse = jnp.where(any_live, row_max + jnp.log(safe), NEG_FILL)
    mean = jnp.where(any_live, stats[2] / safe, 0.0)
    stat_send[...] = jnp.where(left, lse, pltpu.roll(mean, 64, 1))
    stat_g[c] = stat_send[...]
    spread(stat_send, stat_g, "col", 3)
    wait_recv(stat_g, 3)
    top = stat_g[0]
    for s in range(1, PEERS):
        top = jnp.maximum(top, stat_g[s])
    total = jnp.zeros((HP, 128), F32)
    dsum = jnp.zeros((HP, 128), F32)
    for s in range(PEERS):
        got = stat_g[s]
        weight = jnp.exp(got - top)
        total = total + weight
        dsum = dsum + weight * pltpu.roll(got, 64, 1)
    stats[0] = jnp.exp(row_max - top) / total
    stats[1] = dsum / total

    @pl.loop(0, 8, unroll=8)
    def _(b):
        scale = pltpu.roll(stats[0], lax.rem(128 - 8 * b, 128), 1)
        mean_all = pltpu.roll(stats[1], lax.rem(128 - 8 * b, 128), 1)
        for i in range(4):
            rows = pl.ds(64 * b + 16 * i, 16)
            factor = jnp.where(left, scale[:, 2 * i : 2 * i + 1], scale[:, 2 * i + 1 : 2 * i + 2])
            shift = jnp.where(left, mean_all[:, 2 * i : 2 * i + 1], mean_all[:, 2 * i + 1 : 2 * i + 2])
            p = expo[rows, :] * factor
            ds = p * (dprob[rows, :] - shift)
            high, low = split(ds)
            prob[rows, :] = p.astype(BF16).astype(F32)
            dsr[rows, :] = high.astype(F32)
            dlo[rows, :] = low

    def weight_step(t, acc):
        high = dsr[pl.ds(32 * t, 32), :].astype(BF16)
        low = dlo[pl.ds(32 * t, 32), :]
        lhs = jnp.concatenate(
            (
                jnp.concatenate((high[0:16], high[16:32]), 1),
                jnp.concatenate((low[0:16], low[16:32]), 1),
            ),
            0,
        )
        return acc + nn(lhs, pp[pl.ds(256 * t, 256), :])

    w_all = lax.fori_loop(0, 16, weight_step, jnp.zeros((2 * HP, 256), F32), unroll=16)
    w_all = w_all[:, 0:128] + w_all[:, 128:256]
    w_send[...] = W_LOGIT * (w_all[0:HP] + w_all[HP : 2 * HP])
    w_row[r] = w_send[...]
    spread(w_send, w_row, "row", 4)

    ds_t = jnp.transpose(dsr[...]).astype(BF16)
    prob_t = jnp.transpose(prob[...]).astype(BF16)
    kside = nn(ds_t[0:TILE], qbd[0, :, 0:512]) + nn(ds_t[TILE : 2 * TILE], qbd[1, :, 0:512])
    vside = nn(prob_t[0:TILE], qbd[0, :, 512:1024]) + nn(prob_t[TILE : 2 * TILE], qbd[1, :, 512:1024])
    expand_q = jnp.concatenate((jnp.zeros((64, 256), F32), point_mask, jnp.zeros((48, 256), F32)), 0)
    expand_k = jnp.concatenate((jnp.zeros((80, 256), F32), point_mask, jnp.zeros((32, 256), F32)), 0)
    ps_row = jnp.concatenate(ps_lane, 1)
    kres[:, 0:256] = SCALE_Q * kside[:, 0:256]
    kres[:, 256:512] = -2.0 * ps_row * (
        exact_nn(kside[:, 128:256], expand_q) * kf[:, 256:512] - kside[:, 256:512]
    )
    kres[:, 512:1024] = vside
    for s in range(PEERS):
        for t in range(8):
            kch[s, 4 * t : 4 * t + 4, :] = kres[4 * s : 4 * s + 4, 128 * t : 128 * t + 128]
    kr[r] = kch[r]
    scatter(kch, kr, "row", 5)

    left32 = lax.broadcasted_iota(jnp.int32, (32, 128), 1) < 64
    evens, odds = [], []
    for pairing in range(H // 2):
        one = dsr[pl.ds(2 * pairing, 32, stride=HP), :]
        two = dsr[pl.ds(2 * pairing + 1, 32, stride=HP), :]
        evens.append(jnp.where(left32, one, pltpu.roll(two, 64, 1)).astype(BF16))
        odds.append(jnp.where(left32, pltpu.roll(one, 64, 1), two).astype(BF16))
    lhs = jnp.concatenate((jnp.concatenate(evens, 1), jnp.concatenate(odds, 1)), 0)
    qside = nn(lhs, kbd[...])
    for t in range(4):
        for odd in range(2):
            qres[t, pl.ds(odd, 32, stride=2), :] = qside[32 * odd : 32 * odd + 32, 128 * t : 128 * t + 128]
    row_sums = exact_nn(qres[1], expand_k)
    for t in (2, 3):
        at = 128 * (t - 2)
        qres[t] = -2.0 * ps_lane[t - 2] * (
            row_sums[:, at : at + 128] * qf[:, 128 * t : 128 * t + 128] - qres[t]
        )
    for t in (0, 1):
        qres[t] = SCALE_Q * qres[t]
    for s in range(PEERS):
        for t in range(4):
            qch[s, 4 * t : 4 * t + 4, :] = qres[t, 4 * s : 4 * s + 4, :]
    qr[c] = qch[c]
    scatter(qch, qr, "col", 6)

    wait_recv(w_row, 4)
    w_sum = w_row[0]
    for s in range(1, PEERS):
        w_sum = w_sum + w_row[s]
    w_mid[...] = w_sum
    w_col[c] = w_sum
    spread(w_mid, w_col, "col", 7)

    wb = jnp.concatenate((wb_high, wb_high, wb_low), 0)
    @pl.loop(0, 16, unroll=16)
    def _(t):
        gz = gzp[t]
        for a in range(2):
            rows = pl.ds(32 * t + 16 * a, 16)
            p = prob[rows, :]
            high = dsr[rows, :].astype(BF16)
            lhs = jnp.concatenate(
                (
                    jnp.where(left, p, 0.0).astype(BF16),
                    jnp.where(left, 0.0, p).astype(BF16),
                    high,
                    dlo[rows, :],
                    high,
                ),
                0,
            )
            rhs = jnp.concatenate((gz[32 * a : 32 * a + 32], wb), 0)
            gpair_out[pl.ds(256 * t + 128 * a, 128), :] = tn(lhs, rhs)

    wait_recv(kr, 5)
    ksum = kr[0]
    for s in range(1, PEERS):
        ksum = ksum + kr[s]
    gk_out[:, 0:128] = ksum[0:4]
    gk_out[:, 128:192] = ksum[4:8, 0:64]
    gkp_out[:, 0:128] = ksum[8:12]
    gkp_out[:, 128:144] = ksum[12:16, 0:16]
    gv_out[:, 0:128] = ksum[16:20]
    gv_out[:, 128:192] = ksum[28:32, 0:64]
    gvp_out[:, 0:128] = ksum[20:24]
    gvp_out[:, 128:256] = ksum[24:28]
    gvp_out[:, 256:288] = ksum[28:32, 64:96]
    wait_recv(qr, 6)
    qsum = qr[0]
    for s in range(1, PEERS):
        qsum = qsum + qr[s]
    gq_out[:, 0:128] = qsum[0:4]
    gq_out[:, 128:192] = qsum[4:8, 0:64]
    gqp_out[:, 0:128] = qsum[8:12]
    gqp_out[:, 128:144] = qsum[12:16, 0:16]


    wait_recv(w_col, 7)
    w_sum = w_col[0]
    for s in range(1, PEERS):
        w_sum = w_sum + w_col[s]
    gbw_out[...] = w_sum[0:H]

    for n, dst in enumerate((qg, kg, gzg, stat_g, w_row, kr, qr, w_col)):
        wait_send(dst, n)


def finish(*refs):
    sem = refs[-1]
    copies = [pltpu.make_async_copy(refs[n], refs[8 + n], sem.at[n]) for n in range(8)]
    for copy in copies:
        copy.start()
    for copy in copies:
        copy.wait()


def on_device(
    queries, query_points, key_feats, key_points, values, value_points, pair_rep, bias_weight,
    head_weight, chain_bias, chain_ids, live_mask, cot_scalar, cot_points, cot_pair,
):
    any_spec = pl.BlockSpec(memory_space=pl.ANY)
    vmem_spec = pl.BlockSpec(memory_space=pltpu.VMEM)

    def vm(*shape, kind=F32):
        return pltpu.VMEM(shape, kind)

    scratch = [
        vm(4, 192, kind=BF16), vm(4, 144, kind=BF16), vm(4, 192, kind=BF16), vm(4, 144, kind=BF16),
        vm(4, 192, kind=BF16), vm(4, 288, kind=BF16), vm(4096, 128), vm(H, 128),
        pltpu.SMEM((H,), F32), pltpu.SMEM((H,), F32),
        pltpu.SMEM((8, 128), jnp.int32), pltpu.SMEM((8, 128), jnp.int32),
        vm(8, 128, kind=jnp.int32), vm(8, 128, kind=jnp.int32),
        vm(4, 192, kind=BF16), vm(4, 288, kind=BF16), vm(4, 1536, kind=BF16),
        vm(32, 128), vm(4 * H, 128), vm(32, 128, kind=BF16), vm(32, 128, kind=BF16), vm(4 * H, 128, kind=BF16),
        vm(PEERS, 32, 128, kind=BF16), vm(PEERS, 32, 128, kind=BF16), vm(PEERS, 4 * H, 128, kind=BF16),
        vm(PEERS, 32, 128), vm(PEERS * 4 * H, 128), vm(PEERS * 4 * HP, 128), vm(PEERS, 4 * HP, 128, kind=BF16),
        vm(TILE, 1024), vm(TILE, 1024), vm(1024, 128, kind=BF16), vm(2, 512, 1024, kind=BF16),
        vm(H * TILE, 512, kind=BF16), vm(4096, 256, kind=BF16), vm(16, 256, 256, kind=BF16), vm(512, 128), vm(512, 128), vm(512, 128),
        vm(512, 128), vm(512, 128), vm(512, 128), vm(512, 128, kind=BF16),
        vm(3, HP, 128), vm(HP, 128), vm(PEERS, HP, 128), vm(HP, 128), vm(PEERS, HP, 128), vm(HP, 128),
        vm(PEERS, HP, 128),
        vm(TILE, 1024), vm(PEERS, 32, 128), vm(PEERS, 32, 128), vm(4, TILE, 128), vm(PEERS, 16, 128),
        vm(PEERS, 16, 128),
        pltpu.SemaphoreType.DMA((17,)),
        pltpu.SemaphoreType.DMA((8,)), pltpu.SemaphoreType.DMA((8,)),
    ]
    out_shape = [
        jax.ShapeDtypeStruct(shape, F32)
        for shape in ((4, 192), (4, 144), (4, 192), (4, 144), (4, 192), (4, 288), (4096, 128), (H, 128))
    ]
    out = pl.pallas_call(
        kernel,
        out_shape=[pltpu.VMEM(shape.shape, F32) for shape in out_shape],
        in_specs=[any_spec] * 15,
        out_specs=[vmem_spec] * 8,
        scratch_shapes=scratch,
        compiler_params=pltpu.CompilerParams(
            collective_id=0, has_side_effects=True, vmem_limit_bytes=VMEM_LIMIT
        ),
        cost_estimate=pl.CostEstimate(flops=10**9, bytes_accessed=5 * 2**20, transcendentals=10**5),
    )(*(pltpu.with_memory_space_constraint(x, pltpu.HBM) for x in (
        queries, query_points, key_feats, key_points, values, value_points,
        pair_rep.reshape(4096, 128), bias_weight.T, head_weight, chain_bias,
        chain_ids.reshape(8, 128), live_mask.reshape(8, 128), cot_scalar, cot_points, cot_pair,
    )))
    out = pl.pallas_call(
        finish,
        out_shape=out_shape,
        in_specs=[vmem_spec] * 8,
        out_specs=[any_spec] * 8,
        scratch_shapes=[pltpu.SemaphoreType.DMA((8,))],
        compiler_params=pltpu.CompilerParams(vmem_limit_bytes=2**20),
    )(*out)
    return (*out[:6], out[6].reshape(TILE, TILE, 128), out[7].T)


def solution(mesh):
    rc, cr = P(("row", "col"), None), P(("col", "row"), None)
    tile = P("row", "col", None)
    return jax.shard_map(
        on_device,
        mesh=mesh,
        in_specs=(rc, rc, cr, cr, cr, cr, tile, P(), P(), P(), P(), P(), rc, rc, rc),
        out_specs=(rc, rc, cr, cr, cr, cr, tile, P()),
        check_vma=False,
    )
```

```python
import math

import jax
import jax.numpy as jnp
from jax import lax
from jax.experimental import pallas as pl
from jax.experimental.pallas import tpu as pltpu
from jax.sharding import PartitionSpec as P

MESH = pl.DeviceIdType.MESH
NEG_FILL = -1e30
F32 = jnp.float32
BF16 = jnp.bfloat16
H = 12
HP = 16
TILE = 64
PEERS = 16
VMEM_LIMIT = 40 * 2**20
PIECES = 8
W_LOGIT = math.sqrt(1.0 / 3.0)
W_POINT = math.sqrt(2.0 / 36.0)
SCALE_Q = W_LOGIT / 4.0


def nn(a, b):
    return lax.dot_general(a, b, (((1,), (0,)), ((), ())), preferred_element_type=F32)


def tn(a, b):
    return lax.dot_general(a, b, (((0,), (0,)), ((), ())), preferred_element_type=F32)


def exact_nn(a, b):
    return lax.dot_general(
        a, b, (((1,), (0,)), ((), ())), preferred_element_type=F32, precision=lax.Precision.HIGHEST
    )


def split(x):
    high = x.astype(BF16)
    return high, (x - high.astype(F32)).astype(BF16)


def head_masks(sub, lane):
    def block(col, width):
        return (col >= sub * width) & (col < sub * width + width)

    tiles = [
        block(lane, 16),
        ((lane < 64) & block(lane + 128, 16)) | (lane == sub + 64) | (lane == sub + 80),
        block(lane, 12),
        (lane < 16) & block(lane + 128, 12),
        block(lane, 16),
        block(lane, 24),
        block(lane + 128, 24),
        ((lane < 64) & block(lane + 128, 16)) | ((lane >= 64) & (lane < 96) & block(lane + 192, 24)),
    ]
    return [(tile & (sub < H)).astype(F32) for tile in tiles]


def kernel(
    q_in, qp_in, k_in, kp_in, v_in, vp_in, pair_in, bw_in, hw_in, cb_in, chain_in, live_in,
    gs_in, gp_in, gz_in,
    gq_out, gqp_out, gk_out, gkp_out, gv_out, gvp_out, gpair_out, gbw_out,
    q_v, qp_v, k_v, kp_v, v_v, vp_v, pair_v, bw_v, hw_s, cb_s, chain_s, live_s, chain_v, live_v,
    gs_v, gp_v, gz_v,
    pack, gz32, qsend, ksend, gzsend, qg, kg, gzg, blk, gz12, gz16, gzp,
    qf, kf, kdup, qbd, kbd, pp, ppt, sums_xy, base, qsq, expo, dprob, prob, dsr, dlo,
    stats, stat_send, stat_g, w_send, w_row, w_mid, w_col,
    kres, kch, kr, qres, qch, qr,
    in_sem, send_sem, recv_sem,
):
    r = lax.axis_index("row")
    c = lax.axis_index("col")
    barrier = pltpu.get_barrier_semaphore()

    def fan(axis, act):
        if axis == "col":
            y, z = c // 8, lax.rem(c, 8)

            def at(dy, j):
                dz = 4 + (1 - 2 * lax.rem(j, 2)) * ((j + 1) // 2)
                act((r, lax.rem(y + dy, 2) * 8 + lax.rem(z + dz, 8)))

            @pl.loop(0, 3, unroll=3)
            def _(j):
                at(1, j)

            @pl.loop(3, 8, unroll=5)
            def _(j):
                at(1, j)
                at(0, j - 3)

            @pl.loop(5, 7, unroll=2)
            def _(j):
                at(0, j)
        else:
            x, y, core = r // 4, lax.rem(r // 2, 2), lax.rem(r, 2)

            def at(dx, dy, dc):
                act((lax.rem(x + dx, 4) * 4 + lax.rem(y + dy, 2) * 2 + lax.rem(core + dc, 2), c))

            @pl.loop(0, 3, unroll=3)
            def _(m):
                dx = 2 + (1 - 2 * lax.rem(m, 2)) * ((m + 1) // 2)
                at(dx, 1, 1)
                at(dx, 1, 0)
                at(dx, 0, 1)
                at(dx, 0, 0)

            at(0, 1, 1)
            at(0, 1, 0)
            at(0, 0, 1)

    def greet(peer):
        pl.semaphore_signal(barrier, inc=1, device_id=peer, device_id_type=MESH)

    fan("col", greet)
    fan("row", greet)

    loads = [
        pltpu.make_async_copy(src, dst, in_sem.at[n])
        for n, (src, dst) in enumerate(
            (
                (pair_in, pair_v), (q_in, q_v), (qp_in, qp_v), (k_in, k_v), (kp_in, kp_v), (v_in, v_v),
                (vp_in, vp_v), (bw_in, bw_v), (hw_in, hw_s), (cb_in, cb_s), (chain_in, chain_s),
                (live_in, live_s), (chain_in, chain_v), (live_in, live_v), (gs_in, gs_v), (gp_in, gp_v),
                (gz_in, gz_v),
            )
        )
    ]
    for load in loads[1:]:
        load.start()
    loads[0].start()
    for load in loads[1:]:
        load.wait()

    sub = lax.broadcasted_iota(jnp.int32, (HP, 128), 0)
    lane = lax.broadcasted_iota(jnp.int32, (HP, 128), 1)
    left = lane < 64
    masks = head_masks(sub, lane)

    gz16[...] = jnp.zeros_like(gz16)

    live4 = jnp.zeros((4, 128), F32)
    sub4 = lax.broadcasted_iota(jnp.int32, (4, 128), 0)
    first = r * TILE + c * 4
    for i in range(4):
        at = first + i
        live4 = jnp.where(sub4 == i, live_s[at // 128, lax.rem(at, 128)].astype(F32), live4)

    def pack_block(scalars, points, vals, vpoints, ones, live, send):
        pack[...] = jnp.zeros_like(pack)
        a, b = scalars[...].astype(F32), points[...].astype(F32)
        d, e = vals[...].astype(F32), vpoints[...].astype(F32)
        pack[0:4, :] = a[:, 0:128]
        pack[4:8, 0:64] = a[:, 128:192]
        pack[4:8, ones : ones + 16] = jnp.ones((4, 16), F32)
        pack[8:12, :] = b[:, 0:128]
        pack[12:16, 0:16] = b[:, 128:144]
        pack[16:20, :] = d[:, 0:128] * live
        pack[20:24, :] = e[:, 0:128] * live
        pack[24:28, :] = e[:, 128:256] * live
        pack[28:32, 0:64] = d[:, 128:192] * live[:, 0:64]
        pack[28:32, 64:96] = e[:, 256:288] * live[:, 0:32]
        send[...] = pack[...].astype(BF16)

    pack_block(q_v, qp_v, gs_v, gp_v, 64, live4, qsend)
    pack_block(k_v, kp_v, v_v, vp_v, 80, jnp.ones((4, 128), F32), ksend)
    for h in range(H):
        gz32[pl.ds(h, 4, stride=H), :] = gz_v[:, 128 * h : 128 * h + 128].astype(F32) * live4
    gzsend[...] = gz32[...].astype(BF16)
    qg[c] = qsend[...]
    kg[r] = ksend[...]
    gzg[c] = gzsend[...]

    ps = jnp.zeros((HP, 128), F32)
    cb = jnp.zeros((HP, 128), F32)
    for h in range(H):
        ps = jnp.where(sub == h, hw_s[h], ps)
        cb = jnp.where(sub == h, cb_s[h], cb)
    ps = W_LOGIT * ps * W_POINT / 2.0
    ps_lane = [jnp.sum(masks[t] * ps, 0, keepdims=True) for t in (2, 3)]
    bw_t = jnp.concatenate((bw_v[...], jnp.zeros((HP - H, 128), F32)), 0)
    bw_high, bw_low = split(bw_t)
    wb_high, wb_low = split(W_LOGIT * bw_t)
    col_at = c * TILE
    chain_k = chain_v[pl.ds(col_at // 128, 1), :]
    live_k = live_v[pl.ds(col_at // 128, 1), :].astype(F32)
    half = lax.rem(c, 2)
    lane1 = lax.broadcasted_iota(jnp.int32, (1, 128), 1)
    own = (lane1 // 64) == half
    chain_k = jnp.where(own, chain_k, pltpu.roll(chain_k, 64, 1))
    live_k = jnp.where(own, live_k, pltpu.roll(live_k, 64, 1))

    pl.semaphore_wait(barrier, 2 * (PEERS - 1))

    def spread(src, dst, axis, n):
        me = c if axis == "col" else r

        def act(peer):
            pltpu.make_async_remote_copy(
                src_ref=src,
                dst_ref=dst.at[me],
                send_sem=send_sem.at[n],
                recv_sem=recv_sem.at[n],
                device_id=peer,
                device_id_type=MESH,
            ).start()

        fan(axis, act)

    def scatter(src, dst, axis, n):
        me = c if axis == "col" else r

        def act(peer):
            pltpu.make_async_remote_copy(
                src_ref=src.at[peer[1] if axis == "col" else peer[0]],
                dst_ref=dst.at[me],
                send_sem=send_sem.at[n],
                recv_sem=recv_sem.at[n],
                device_id=peer,
                device_id_type=MESH,
            ).start()

        fan(axis, act)

    def wait_recv(dst, n):
        part = dst.at[pl.ds(0, PEERS - 1)]
        pltpu.make_async_copy(part, part, recv_sem.at[n]).wait()

    def wait_send(dst, n):
        part = dst.at[pl.ds(0, PEERS - 1)]
        pltpu.make_async_copy(part, part, send_sem.at[n]).wait()

    spread(qsend, qg, "col", 0)
    spread(ksend, kg, "row", 1)
    spread(gzsend, gzg, "col", 2)

    loads[0].wait()
    bias_lhs = jnp.concatenate(
        (jnp.concatenate((bw_high, bw_high), 1), jnp.concatenate((bw_low, bw_low), 1)), 0
    )

    @pl.loop(0, 16)
    def _(t):
        high, low = split(pair_v[pl.ds(256 * t, 256), :])
        both = jnp.concatenate((high, low), 1)
        pp[pl.ds(256 * t, 256), :] = both
        both_t = jnp.transpose(both)
        ppt[t] = both_t
        res = nn(bias_lhs, both_t)
        res = res[0:HP] + res[HP : 2 * HP]
        for a in range(2):
            at = r * TILE + 4 * t + 2 * a
            chain_q = jnp.where(
                lane1 < 64, chain_s[at // 128, lax.rem(at, 128)], chain_s[(at + 1) // 128, lax.rem(at + 1, 128)]
            )
            same = (chain_q == chain_k).astype(F32)
            base[pl.ds(32 * t + 16 * a, 16), :] = W_LOGIT * (res[:, 128 * a : 128 * a + 128] + cb * same)

    def assemble(got, full):
        blk[...] = got[...].astype(F32)
        for s in range(PEERS):
            for t in range(8):
                full[4 * s : 4 * s + 4, 128 * t : 128 * t + 128] = blk[s, 4 * t : 4 * t + 4, :]

    wait_recv(kg, 1)
    assemble(kg, kf)
    k_t = jnp.transpose(kf[...])
    k_t = jnp.concatenate((k_t, k_t), 1)
    kdup[...] = k_t.astype(BF16)
    point_mask = jnp.concatenate((masks[2], masks[3]), 1)
    point_mask16 = point_mask.astype(BF16)
    square_high, square_low = split(k_t[256:512] * k_t[256:512])
    k_sq = nn(point_mask16, square_high) + nn(point_mask16, square_low)

    wait_recv(qg, 0)

    @pl.loop(0, PEERS, unroll=PEERS)
    def _(s):
        got = qg[s].astype(F32)
        for p in range(2):
            rows = pl.ds(32 * s + HP * p, HP)
            sums = []
            for odd in range(2):
                square = jnp.zeros((HP, 128), F32)
                for t in range(8):
                    at = 4 * t + 2 * p + odd
                    value = got[at : at + 1, :] * masks[t]
                    qbd[odd, rows, 128 * t : 128 * t + 128] = value.astype(BF16)
                    if t in (2, 3):
                        square = square + value * value
                sums.append(jnp.sum(square, 1, keepdims=True))
            qsq[rows, :] = jnp.where(left, sums[0], sums[1])

    half_of = lax.broadcasted_iota(jnp.int32, (256, 128), 0) % 128 // 64
    parity = lax.broadcasted_iota(jnp.int32, (256, 128), 1) % 2
    half_ones = (half_of == parity).astype(F32).astype(BF16)

    def half_sums(x):
        return nn(jnp.concatenate(split(x), 1), half_ones)

    lane_pair = lane // 2
    stats[...] = jnp.zeros_like(stats)
    lane3 = lax.broadcasted_iota(jnp.int32, (8, HP, 128), 2)
    left3 = lane3 < 64

    @pl.loop(0, 4, unroll=4)
    def _(b):
        rows = pl.ds(128 * b, 128)
        parts = []
        for k0, k1 in ((0, 256), (256, 512), (512, 1024)):
            both = nn(jnp.concatenate((qbd[0, rows, k0:k1], qbd[1, rows, k0:k1]), 0), kdup[k0:k1, :])
            both = both.reshape(2, 8, HP, 128)
            parts.append(jnp.where(left3, both[0], both[1]))
        dprob[rows, :] = parts[2].reshape(128, 128)
        distance = qsq[rows, :].reshape(8, HP, 128) + k_sq - 2.0 * parts[1]
        logits = base[rows, :].reshape(8, HP, 128) + SCALE_Q * parts[0] - ps * distance
        logits = jnp.where(live_k > 0, logits, NEG_FILL)
        max0 = jnp.max(jnp.where(left3, logits, NEG_FILL), 2, keepdims=True)
        max1 = jnp.max(jnp.where(left3, NEG_FILL, logits), 2, keepdims=True)
        e = jnp.exp(logits - jnp.where(left3, max0, max1)) * live_k
        e = e.reshape(128, 128)
        expo[rows, :] = e
        sums = half_sums(e)
        acc_m, acc_s = stats[0], stats[1]
        for i in range(8):
            at = 16 * b + 2 * i
            acc_m = jnp.where(lane == at, max0[i], jnp.where(lane == at + 1, max1[i], acc_m))
            acc_s = jnp.where(lane_pair == 8 * b + i, sums[HP * i : HP * i + HP], acc_s)
        stats[0] = acc_m
        stats[1] = acc_s

    wait_recv(gzg, 2)

    gz12[...] = gzg[...].astype(F32).reshape(PEERS * 4 * H, 128)

    @pl.loop(0, PEERS, unroll=PEERS)
    def _(t):
        for i in range(4):
            gz16[pl.ds(64 * t + HP * i, H), :] = gz12[pl.ds(48 * t + H * i, H), :]

    gzp[...] = gz16[...].astype(BF16).reshape(PEERS, 4 * HP, 128)

    @pl.loop(0, 16, unroll=16)
    def _(t):
        gz = gzp[t]
        res = nn(jnp.concatenate((gz, gz), 1), ppt[t])
        for a in range(2):
            rows = pl.ds(32 * t + 16 * a, 16)
            tile = res[32 * a : 32 * a + 32, 128 * a : 128 * a + 128]
            dprob[rows, :] = dprob[rows, :] + jnp.where(left, tile[0:16], tile[16:32])

    sums = half_sums(expo[...] * dprob[...])
    acc = jnp.zeros((HP, 128), F32)
    for p in range(32):
        acc = jnp.where(lane_pair == p, sums[HP * p : HP * p + HP], acc)
    stats[2] = acc

    row_max, row_sum = stats[0], stats[1]
    any_live = row_sum > 0
    safe = jnp.where(any_live, row_sum, 1.0)
    lse = jnp.where(any_live, row_max + jnp.log(safe), NEG_FILL)
    mean = jnp.where(any_live, stats[2] / safe, 0.0)
    stat_send[...] = jnp.where(left, lse, pltpu.roll(mean, 64, 1))
    stat_g[c] = stat_send[...]
    spread(stat_send, stat_g, "col", 3)
    assemble(qg, qf)
    for h in range(H):
        for t in range(4):
            kbd[TILE * h : TILE * h + TILE, 128 * t : 128 * t + 128] = (
                kf[:, 128 * t : 128 * t + 128] * masks[t][h : h + 1, :]
            ).astype(BF16)

    @pl.loop(0, 32, unroll=8)
    def _(p):
        rows = pl.ds(pl.multiple_of(HP * p, HP), HP)
        e = expo[rows, :]
        terms = []
        for side in (left, jnp.logical_not(left)):
            own = jnp.where(side, e, 0.0)
            terms += [*split(own * dprob[rows, :]), *split(own)]
        res = nn(jnp.concatenate(terms, 0), pp[pl.ds(pl.multiple_of(128 * p, 128), 128), :])
        res = res[:, 0:128] + res[:, 128:256]
        for n in range(4):
            sums_xy[p, n] = res[32 * n : 32 * n + 16] + res[32 * n + 16 : 32 * n + 32]

    wait_recv(stat_g, 3)
    top = stat_g[0]
    for s in range(1, PEERS):
        top = jnp.maximum(top, stat_g[s])
    total = jnp.zeros((HP, 128), F32)
    dsum = jnp.zeros((HP, 128), F32)
    for s in range(PEERS):
        got = stat_g[s]
        weight = jnp.exp(got - top)
        total = total + weight
        dsum = dsum + weight * pltpu.roll(got, 64, 1)
    scales = jnp.exp(row_max - top) / total
    means = dsum / total
    stats[0] = scales
    stats[1] = means

    shifts = scales * means
    w_parts = []
    for p in range(32):
        part = jnp.zeros((HP, 128), F32)
        for odd in range(2):
            i = 2 * p + odd
            part = part + scales[:, i : i + 1] * sums_xy[p, 2 * odd] - shifts[:, i : i + 1] * sums_xy[p, 2 * odd + 1]
        w_parts.append(part)
    while len(w_parts) > 1:
        w_parts = [one + two for one, two in zip(w_parts[0::2], w_parts[1::2])]
    w_send[...] = W_LOGIT * w_parts[0]
    w_row[r] = w_send[...]
    spread(w_send, w_row, "row", 4)

    @pl.loop(0, 8, unroll=8)
    def _(b):
        scale = pltpu.roll(stats[0], lax.rem(128 - 8 * b, 128), 1)
        mean_all = pltpu.roll(stats[1], lax.rem(128 - 8 * b, 128), 1)
        for i in range(4):
            rows = pl.ds(64 * b + 16 * i, 16)
            factor = jnp.where(left, scale[:, 2 * i : 2 * i + 1], scale[:, 2 * i + 1 : 2 * i + 2])
            shift = jnp.where(left, mean_all[:, 2 * i : 2 * i + 1], mean_all[:, 2 * i + 1 : 2 * i + 2])
            p = expo[rows, :] * factor
            ds = p * (dprob[rows, :] - shift)
            high, low = split(ds)
            prob[rows, :] = p.astype(BF16).astype(F32)
            dsr[rows, :] = high.astype(F32)
            dlo[rows, :] = low

    ds_t = jnp.transpose(dsr[...]).astype(BF16)
    prob_t = jnp.transpose(prob[...]).astype(BF16)
    kside = nn(ds_t[0:TILE], qbd[0, :, 0:512]) + nn(ds_t[TILE : 2 * TILE], qbd[1, :, 0:512])
    vside = nn(prob_t[0:TILE], qbd[0, :, 512:1024]) + nn(prob_t[TILE : 2 * TILE], qbd[1, :, 512:1024])
    expand_q = jnp.concatenate((jnp.zeros((64, 256), F32), point_mask, jnp.zeros((48, 256), F32)), 0)
    expand_k = jnp.concatenate((jnp.zeros((80, 256), F32), point_mask, jnp.zeros((32, 256), F32)), 0)
    ps_row = jnp.concatenate(ps_lane, 1)
    kres[:, 0:256] = SCALE_Q * kside[:, 0:256]
    kres[:, 256:512] = -2.0 * ps_row * (
        exact_nn(kside[:, 128:256], expand_q) * kf[:, 256:512] - kside[:, 256:512]
    )
    kres[:, 512:1024] = vside
    for s in range(PEERS):
        for t in range(8):
            kch[s, 4 * t : 4 * t + 4, :] = kres[4 * s : 4 * s + 4, 128 * t : 128 * t + 128]
    kr[r] = kch[r]
    scatter(kch, kr, "row", 5)

    left32 = lax.broadcasted_iota(jnp.int32, (32, 128), 1) < 64
    evens, odds = [], []
    for pairing in range(H // 2):
        one = dsr[pl.ds(2 * pairing, 32, stride=HP), :]
        two = dsr[pl.ds(2 * pairing + 1, 32, stride=HP), :]
        evens.append(jnp.where(left32, one, pltpu.roll(two, 64, 1)).astype(BF16))
        odds.append(jnp.where(left32, pltpu.roll(one, 64, 1), two).astype(BF16))
    lhs = jnp.concatenate((jnp.concatenate(evens, 1), jnp.concatenate(odds, 1)), 0)
    qside = nn(lhs, kbd[...])
    for t in range(4):
        for odd in range(2):
            qres[t, pl.ds(odd, 32, stride=2), :] = qside[32 * odd : 32 * odd + 32, 128 * t : 128 * t + 128]
    row_sums = exact_nn(qres[1], expand_k)
    for t in (2, 3):
        at = 128 * (t - 2)
        qres[t] = -2.0 * ps_lane[t - 2] * (
            row_sums[:, at : at + 128] * qf[:, 128 * t : 128 * t + 128] - qres[t]
        )
    for t in (0, 1):
        qres[t] = SCALE_Q * qres[t]
    for s in range(PEERS):
        for t in range(4):
            qch[s, 4 * t : 4 * t + 4, :] = qres[t, 4 * s : 4 * s + 4, :]
    qr[c] = qch[c]
    scatter(qch, qr, "col", 6)

    wait_recv(w_row, 4)
    w_sum = w_row[0]
    for s in range(1, PEERS):
        w_sum = w_sum + w_row[s]
    w_mid[...] = w_sum
    w_col[c] = w_sum
    spread(w_mid, w_col, "col", 7)

    wb = jnp.concatenate((wb_high, wb_high, wb_low), 0)
    @pl.loop(0, 16, unroll=16)
    def _(t):
        gz = gzp[t]
        for a in range(2):
            rows = pl.ds(32 * t + 16 * a, 16)
            p = prob[rows, :]
            high = dsr[rows, :].astype(BF16)
            lhs = jnp.concatenate(
                (
                    jnp.where(left, p, 0.0).astype(BF16),
                    jnp.where(left, 0.0, p).astype(BF16),
                    high,
                    dlo[rows, :],
                    high,
                ),
                0,
            )
            rhs = jnp.concatenate((gz[32 * a : 32 * a + 32], wb), 0)
            gpair_out[pl.ds(256 * t + 128 * a, 128), :] = tn(lhs, rhs)

    wait_recv(kr, 5)
    ksum = kr[0]
    for s in range(1, PEERS):
        ksum = ksum + kr[s]
    gk_out[:, 0:128] = ksum[0:4]
    gk_out[:, 128:192] = ksum[4:8, 0:64]
    gkp_out[:, 0:128] = ksum[8:12]
    gkp_out[:, 128:144] = ksum[12:16, 0:16]
    gv_out[:, 0:128] = ksum[16:20]
    gv_out[:, 128:192] = ksum[28:32, 0:64]
    gvp_out[:, 0:128] = ksum[20:24]
    gvp_out[:, 128:256] = ksum[24:28]
    gvp_out[:, 256:288] = ksum[28:32, 64:96]
    wait_recv(qr, 6)
    qsum = qr[0]
    for s in range(1, PEERS):
        qsum = qsum + qr[s]
    gq_out[:, 0:128] = qsum[0:4]
    gq_out[:, 128:192] = qsum[4:8, 0:64]
    gqp_out[:, 0:128] = qsum[8:12]
    gqp_out[:, 128:144] = qsum[12:16, 0:16]


    wait_recv(w_col, 7)
    w_sum = w_col[0]
    for s in range(1, PEERS):
        w_sum = w_sum + w_col[s]
    gbw_out[...] = w_sum[0:H]

    for n, dst in enumerate((qg, kg, gzg, stat_g, w_row, kr, qr, w_col)):
        wait_send(dst, n)


def finish(*refs):
    sem = refs[-1]
    rows = 4096 // PIECES
    pairs = [(refs[6].at[pl.ds(rows * n, rows)], refs[14].at[pl.ds(rows * n, rows)]) for n in range(PIECES)]
    pairs += [(refs[n], refs[8 + n]) for n in range(8) if n != 6]
    copies = [pltpu.make_async_copy(src, dst, sem.at[n]) for n, (src, dst) in enumerate(pairs)]
    for copy in copies:
        copy.start()
    for copy in copies:
        copy.wait()


def on_device(
    queries, query_points, key_feats, key_points, values, value_points, pair_rep, bias_weight,
    head_weight, chain_bias, chain_ids, live_mask, cot_scalar, cot_points, cot_pair,
):
    any_spec = pl.BlockSpec(memory_space=pl.ANY)
    vmem_spec = pl.BlockSpec(memory_space=pltpu.VMEM)

    def vm(*shape, kind=F32):
        return pltpu.VMEM(shape, kind)

    scratch = [
        vm(4, 192, kind=BF16), vm(4, 144, kind=BF16), vm(4, 192, kind=BF16), vm(4, 144, kind=BF16),
        vm(4, 192, kind=BF16), vm(4, 288, kind=BF16), vm(4096, 128), vm(H, 128),
        pltpu.SMEM((H,), F32), pltpu.SMEM((H,), F32),
        pltpu.SMEM((8, 128), jnp.int32), pltpu.SMEM((8, 128), jnp.int32),
        vm(8, 128, kind=jnp.int32), vm(8, 128, kind=jnp.int32),
        vm(4, 192, kind=BF16), vm(4, 288, kind=BF16), vm(4, 1536, kind=BF16),
        vm(32, 128), vm(4 * H, 128), vm(32, 128, kind=BF16), vm(32, 128, kind=BF16), vm(4 * H, 128, kind=BF16),
        vm(PEERS, 32, 128, kind=BF16), vm(PEERS, 32, 128, kind=BF16), vm(PEERS, 4 * H, 128, kind=BF16),
        vm(PEERS, 32, 128), vm(PEERS * 4 * H, 128), vm(PEERS * 4 * HP, 128), vm(PEERS, 4 * HP, 128, kind=BF16),
        vm(TILE, 1024), vm(TILE, 1024), vm(1024, 128, kind=BF16), vm(2, 512, 1024, kind=BF16),
        vm(H * TILE, 512, kind=BF16), vm(4096, 256, kind=BF16), vm(16, 256, 256, kind=BF16), vm(32, 4, HP, 128), vm(512, 128), vm(512, 128), vm(512, 128),
        vm(512, 128), vm(512, 128), vm(512, 128), vm(512, 128, kind=BF16),
        vm(3, HP, 128), vm(HP, 128), vm(PEERS, HP, 128), vm(HP, 128), vm(PEERS, HP, 128), vm(HP, 128),
        vm(PEERS, HP, 128),
        vm(TILE, 1024), vm(PEERS, 32, 128), vm(PEERS, 32, 128), vm(4, TILE, 128), vm(PEERS, 16, 128),
        vm(PEERS, 16, 128),
        pltpu.SemaphoreType.DMA((17,)),
        pltpu.SemaphoreType.DMA((8,)), pltpu.SemaphoreType.DMA((8,)),
    ]
    out_shape = [
        jax.ShapeDtypeStruct(shape, F32)
        for shape in ((4, 192), (4, 144), (4, 192), (4, 144), (4, 192), (4, 288), (4096, 128), (H, 128))
    ]
    out = pl.pallas_call(
        kernel,
        out_shape=[pltpu.VMEM(shape.shape, F32) for shape in out_shape],
        in_specs=[any_spec] * 15,
        out_specs=[vmem_spec] * 8,
        scratch_shapes=scratch,
        compiler_params=pltpu.CompilerParams(
            collective_id=0, has_side_effects=True, vmem_limit_bytes=VMEM_LIMIT
        ),
        cost_estimate=pl.CostEstimate(flops=10**9, bytes_accessed=5 * 2**20, transcendentals=10**5),
    )(*(pltpu.with_memory_space_constraint(x, pltpu.HBM) for x in (
        queries, query_points, key_feats, key_points, values, value_points,
        pair_rep.reshape(4096, 128), bias_weight.T, head_weight, chain_bias,
        chain_ids.reshape(8, 128), live_mask.reshape(8, 128), cot_scalar, cot_points, cot_pair,
    )))
    out = pl.pallas_call(
        finish,
        out_shape=out_shape,
        in_specs=[vmem_spec] * 8,
        out_specs=[any_spec] * 8,
        scratch_shapes=[pltpu.SemaphoreType.DMA((7 + PIECES,))],
        compiler_params=pltpu.CompilerParams(vmem_limit_bytes=2**20),
    )(*out)
    return (*out[:6], out[6].reshape(TILE, TILE, 128), out[7].T)


def solution(mesh):
    rc, cr = P(("row", "col"), None), P(("col", "row"), None)
    tile = P("row", "col", None)
    return jax.shard_map(
        on_device,
        mesh=mesh,
        in_specs=(rc, rc, cr, cr, cr, cr, tile, P(), P(), P(), P(), P(), rc, rc, rc),
        out_specs=(rc, rc, cr, cr, cr, cr, tile, P()),
        check_vma=False,
    )
```

```python
import math

import jax
import jax.numpy as jnp
from jax import lax
from jax.experimental import pallas as pl
from jax.experimental.pallas import tpu as pltpu
from jax.sharding import PartitionSpec as P

MESH = pl.DeviceIdType.MESH
NEG_FILL = -1e30
F32 = jnp.float32
BF16 = jnp.bfloat16
H = 12
HP = 16
TILE = 64
PEERS = 16
VMEM_LIMIT = 40 * 2**20
W_LOGIT = math.sqrt(1.0 / 3.0)
W_POINT = math.sqrt(2.0 / 36.0)
SCALE_Q = W_LOGIT / 4.0


def nn(a, b):
    return lax.dot_general(a, b, (((1,), (0,)), ((), ())), preferred_element_type=F32)


def tn(a, b):
    return lax.dot_general(a, b, (((0,), (0,)), ((), ())), preferred_element_type=F32)


def exact_nn(a, b):
    return lax.dot_general(
        a, b, (((1,), (0,)), ((), ())), preferred_element_type=F32, precision=lax.Precision.HIGHEST
    )


def split(x):
    high = x.astype(BF16)
    return high, (x - high.astype(F32)).astype(BF16)


def head_masks(sub, lane):
    def block(col, width):
        return (col >= sub * width) & (col < sub * width + width)

    tiles = [
        block(lane, 16),
        ((lane < 64) & block(lane + 128, 16)) | (lane == sub + 64) | (lane == sub + 80),
        block(lane, 12),
        (lane < 16) & block(lane + 128, 12),
        block(lane, 16),
        block(lane, 24),
        block(lane + 128, 24),
        ((lane < 64) & block(lane + 128, 16)) | ((lane >= 64) & (lane < 96) & block(lane + 192, 24)),
    ]
    return [(tile & (sub < H)).astype(F32) for tile in tiles]


def kernel(
    q_in, qp_in, k_in, kp_in, v_in, vp_in, pair_in, bw_in, hw_in, cb_in, chain_in, live_in,
    gs_in, gp_in, gz_in,
    gq_out, gqp_out, gk_out, gkp_out, gv_out, gvp_out, gpair_out, gbw_out,
    q_v, qp_v, k_v, kp_v, v_v, vp_v, pair_v, bw_v, hw_s, cb_s, chain_s, live_s, chain_v, live_v,
    gs_v, gp_v, gz_v,
    pack, gz32, qsend, ksend, gzsend, qg, kg, gzg, blk, gz12, gz16, gzp,
    qf, kf, kdup, qbd, kbd, pp, ppt, sums_xy, base, qsq, expo, dprob, prob, dsr, dlo,
    stats, stat_send, stat_g, w_send, w_row, w_mid, w_col,
    kres, kch, kr, qres, qch, qr,
    in_sem, send_sem, recv_sem,
):
    r = lax.axis_index("row")
    c = lax.axis_index("col")
    barrier = pltpu.get_barrier_semaphore()

    def fan(axis, act):
        if axis == "col":
            y, z = c // 8, lax.rem(c, 8)

            def at(dy, j):
                dz = 4 + (1 - 2 * lax.rem(j, 2)) * ((j + 1) // 2)
                act((r, lax.rem(y + dy, 2) * 8 + lax.rem(z + dz, 8)))

            @pl.loop(0, 3, unroll=3)
            def _(j):
                at(1, j)

            @pl.loop(3, 8, unroll=5)
            def _(j):
                at(1, j)
                at(0, j - 3)

            @pl.loop(5, 7, unroll=2)
            def _(j):
                at(0, j)
        else:
            x, y, core = r // 4, lax.rem(r // 2, 2), lax.rem(r, 2)

            def at(dx, dy, dc):
                act((lax.rem(x + dx, 4) * 4 + lax.rem(y + dy, 2) * 2 + lax.rem(core + dc, 2), c))

            @pl.loop(0, 3, unroll=3)
            def _(m):
                dx = 2 + (1 - 2 * lax.rem(m, 2)) * ((m + 1) // 2)
                at(dx, 1, 1)
                at(dx, 1, 0)
                at(dx, 0, 1)
                at(dx, 0, 0)

            at(0, 1, 1)
            at(0, 1, 0)
            at(0, 0, 1)

    def greet(peer):
        pl.semaphore_signal(barrier, inc=1, device_id=peer, device_id_type=MESH)

    fan("col", greet)
    fan("row", greet)

    loads = [
        pltpu.make_async_copy(src, dst, in_sem.at[n])
        for n, (src, dst) in enumerate(
            (
                (pair_in, pair_v), (q_in, q_v), (qp_in, qp_v), (k_in, k_v), (kp_in, kp_v), (v_in, v_v),
                (vp_in, vp_v), (bw_in, bw_v), (hw_in, hw_s), (cb_in, cb_s), (chain_in, chain_s),
                (live_in, live_s), (chain_in, chain_v), (live_in, live_v), (gs_in, gs_v), (gp_in, gp_v),
                (gz_in, gz_v),
            )
        )
    ]
    for load in loads[1:]:
        load.start()
    loads[0].start()
    for load in loads[1:]:
        load.wait()

    sub = lax.broadcasted_iota(jnp.int32, (HP, 128), 0)
    lane = lax.broadcasted_iota(jnp.int32, (HP, 128), 1)
    left = lane < 64
    masks = head_masks(sub, lane)

    gz16[...] = jnp.zeros_like(gz16)

    live4 = jnp.zeros((4, 128), F32)
    sub4 = lax.broadcasted_iota(jnp.int32, (4, 128), 0)
    first = r * TILE + c * 4
    for i in range(4):
        at = first + i
        live4 = jnp.where(sub4 == i, live_s[at // 128, lax.rem(at, 128)].astype(F32), live4)

    def pack_block(scalars, points, vals, vpoints, ones, live, send):
        pack[...] = jnp.zeros_like(pack)
        a, b = scalars[...].astype(F32), points[...].astype(F32)
        d, e = vals[...].astype(F32), vpoints[...].astype(F32)
        pack[0:4, :] = a[:, 0:128]
        pack[4:8, 0:64] = a[:, 128:192]
        pack[4:8, ones : ones + 16] = jnp.ones((4, 16), F32)
        pack[8:12, :] = b[:, 0:128]
        pack[12:16, 0:16] = b[:, 128:144]
        pack[16:20, :] = d[:, 0:128] * live
        pack[20:24, :] = e[:, 0:128] * live
        pack[24:28, :] = e[:, 128:256] * live
        pack[28:32, 0:64] = d[:, 128:192] * live[:, 0:64]
        pack[28:32, 64:96] = e[:, 256:288] * live[:, 0:32]
        send[...] = pack[...].astype(BF16)

    pack_block(q_v, qp_v, gs_v, gp_v, 64, live4, qsend)
    pack_block(k_v, kp_v, v_v, vp_v, 80, jnp.ones((4, 128), F32), ksend)
    for h in range(H):
        gz32[pl.ds(h, 4, stride=H), :] = gz_v[:, 128 * h : 128 * h + 128].astype(F32) * live4
    gzsend[...] = gz32[...].astype(BF16)
    qg[c] = qsend[...]
    kg[r] = ksend[...]
    gzg[c] = gzsend[...]

    ps = jnp.zeros((HP, 128), F32)
    cb = jnp.zeros((HP, 128), F32)
    for h in range(H):
        ps = jnp.where(sub == h, hw_s[h], ps)
        cb = jnp.where(sub == h, cb_s[h], cb)
    ps = W_LOGIT * ps * W_POINT / 2.0
    ps_lane = [jnp.sum(masks[t] * ps, 0, keepdims=True) for t in (2, 3)]
    bw_t = jnp.concatenate((bw_v[...], jnp.zeros((HP - H, 128), F32)), 0)
    bw_high, bw_low = split(bw_t)
    wb_high, wb_low = split(W_LOGIT * bw_t)
    col_at = c * TILE
    chain_k = chain_v[pl.ds(col_at // 128, 1), :]
    live_k = live_v[pl.ds(col_at // 128, 1), :].astype(F32)
    half = lax.rem(c, 2)
    lane1 = lax.broadcasted_iota(jnp.int32, (1, 128), 1)
    own = (lane1 // 64) == half
    chain_k = jnp.where(own, chain_k, pltpu.roll(chain_k, 64, 1))
    live_k = jnp.where(own, live_k, pltpu.roll(live_k, 64, 1))

    pl.semaphore_wait(barrier, 2 * (PEERS - 1))

    def spread(src, dst, axis, n):
        me = c if axis == "col" else r

        def act(peer):
            pltpu.make_async_remote_copy(
                src_ref=src,
                dst_ref=dst.at[me],
                send_sem=send_sem.at[n],
                recv_sem=recv_sem.at[n],
                device_id=peer,
                device_id_type=MESH,
            ).start()

        fan(axis, act)

    def scatter(src, dst, axis, n):
        me = c if axis == "col" else r

        def act(peer):
            pltpu.make_async_remote_copy(
                src_ref=src.at[peer[1] if axis == "col" else peer[0]],
                dst_ref=dst.at[me],
                send_sem=send_sem.at[n],
                recv_sem=recv_sem.at[n],
                device_id=peer,
                device_id_type=MESH,
            ).start()

        fan(axis, act)

    def wait_recv(dst, n):
        part = dst.at[pl.ds(0, PEERS - 1)]
        pltpu.make_async_copy(part, part, recv_sem.at[n]).wait()

    def wait_send(dst, n):
        part = dst.at[pl.ds(0, PEERS - 1)]
        pltpu.make_async_copy(part, part, send_sem.at[n]).wait()

    spread(qsend, qg, "col", 0)
    spread(ksend, kg, "row", 1)
    spread(gzsend, gzg, "col", 2)

    loads[0].wait()
    bias_lhs = jnp.concatenate(
        (jnp.concatenate((bw_high, bw_high), 1), jnp.concatenate((bw_low, bw_low), 1)), 0
    )

    @pl.loop(0, 16)
    def _(t):
        high, low = split(pair_v[pl.ds(256 * t, 256), :])
        both = jnp.concatenate((high, low), 1)
        pp[pl.ds(256 * t, 256), :] = both
        both_t = jnp.transpose(both)
        ppt[t] = both_t
        res = nn(bias_lhs, both_t)
        res = res[0:HP] + res[HP : 2 * HP]
        for a in range(2):
            at = r * TILE + 4 * t + 2 * a
            chain_q = jnp.where(
                lane1 < 64, chain_s[at // 128, lax.rem(at, 128)], chain_s[(at + 1) // 128, lax.rem(at + 1, 128)]
            )
            same = (chain_q == chain_k).astype(F32)
            base[pl.ds(32 * t + 16 * a, 16), :] = W_LOGIT * (res[:, 128 * a : 128 * a + 128] + cb * same)

    def assemble(got, full):
        blk[...] = got[...].astype(F32)
        for s in range(PEERS):
            for t in range(8):
                full[4 * s : 4 * s + 4, 128 * t : 128 * t + 128] = blk[s, 4 * t : 4 * t + 4, :]

    wait_recv(kg, 1)
    assemble(kg, kf)
    k_t = jnp.transpose(kf[...])
    k_t = jnp.concatenate((k_t, k_t), 1)
    kdup[...] = k_t.astype(BF16)
    point_mask = jnp.concatenate((masks[2], masks[3]), 1)
    point_mask16 = point_mask.astype(BF16)
    square_high, square_low = split(k_t[256:512] * k_t[256:512])
    k_sq = nn(point_mask16, square_high) + nn(point_mask16, square_low)

    wait_recv(qg, 0)

    @pl.loop(0, PEERS, unroll=PEERS)
    def _(s):
        got = qg[s].astype(F32)
        for p in range(2):
            rows = pl.ds(32 * s + HP * p, HP)
            sums = []
            for odd in range(2):
                square = jnp.zeros((HP, 128), F32)
                for t in range(8):
                    at = 4 * t + 2 * p + odd
                    value = got[at : at + 1, :] * masks[t]
                    qbd[odd, rows, 128 * t : 128 * t + 128] = value.astype(BF16)
                    if t in (2, 3):
                        square = square + value * value
                sums.append(jnp.sum(square, 1, keepdims=True))
            qsq[rows, :] = jnp.where(left, sums[0], sums[1])

    half_of = lax.broadcasted_iota(jnp.int32, (256, 128), 0) % 128 // 64
    parity = lax.broadcasted_iota(jnp.int32, (256, 128), 1) % 2
    half_ones = (half_of == parity).astype(F32).astype(BF16)

    def half_sums(x):
        return nn(jnp.concatenate(split(x), 1), half_ones)

    lane_pair = lane // 2
    stats[...] = jnp.zeros_like(stats)
    lane3 = lax.broadcasted_iota(jnp.int32, (8, HP, 128), 2)
    left3 = lane3 < 64

    @pl.loop(0, 4, unroll=4)
    def _(b):
        rows = pl.ds(128 * b, 128)
        parts = []
        for k0, k1 in ((0, 256), (256, 512), (512, 1024)):
            both = nn(jnp.concatenate((qbd[0, rows, k0:k1], qbd[1, rows, k0:k1]), 0), kdup[k0:k1, :])
            both = both.reshape(2, 8, HP, 128)
            parts.append(jnp.where(left3, both[0], both[1]))
        dprob[rows, :] = parts[2].reshape(128, 128)
        distance = qsq[rows, :].reshape(8, HP, 128) + k_sq - 2.0 * parts[1]
        logits = base[rows, :].reshape(8, HP, 128) + SCALE_Q * parts[0] - ps * distance
        logits = jnp.where(live_k > 0, logits, NEG_FILL)
        max0 = jnp.max(jnp.where(left3, logits, NEG_FILL), 2, keepdims=True)
        max1 = jnp.max(jnp.where(left3, NEG_FILL, logits), 2, keepdims=True)
        e = jnp.exp(logits - jnp.where(left3, max0, max1)) * live_k
        e = e.reshape(128, 128)
        expo[rows, :] = e
        sums = half_sums(e)
        acc_m, acc_s = stats[0], stats[1]
        for i in range(8):
            at = 16 * b + 2 * i
            acc_m = jnp.where(lane == at, max0[i], jnp.where(lane == at + 1, max1[i], acc_m))
            acc_s = jnp.where(lane_pair == 8 * b + i, sums[HP * i : HP * i + HP], acc_s)
        stats[0] = acc_m
        stats[1] = acc_s

    row_max, row_sum = stats[0], stats[1]
    any_live = row_sum > 0
    safe = jnp.where(any_live, row_sum, 1.0)
    lse = jnp.where(any_live, row_max + jnp.log(safe), NEG_FILL)
    inverse = 1.0 / safe

    wait_recv(gzg, 2)

    gz12[...] = gzg[...].astype(F32).reshape(PEERS * 4 * H, 128)

    @pl.loop(0, PEERS, unroll=PEERS)
    def _(t):
        for i in range(4):
            gz16[pl.ds(64 * t + HP * i, H), :] = gz12[pl.ds(48 * t + H * i, H), :]

    gzp[...] = gz16[...].astype(BF16).reshape(PEERS, 4 * HP, 128)

    @pl.loop(0, 16, unroll=16)
    def _(t):
        gz = gzp[t]
        res = nn(jnp.concatenate((gz, gz), 1), ppt[t])
        for a in range(2):
            rows = pl.ds(32 * t + 16 * a, 16)
            tile = res[32 * a : 32 * a + 32, 128 * a : 128 * a + 128]
            dprob[rows, :] = dprob[rows, :] + jnp.where(left, tile[0:16], tile[16:32])

    sums = half_sums(expo[...] * dprob[...])
    acc = jnp.zeros((HP, 128), F32)
    for p in range(32):
        acc = jnp.where(lane_pair == p, sums[HP * p : HP * p + HP], acc)
    stats[2] = acc

    mean = jnp.where(any_live, stats[2] * inverse, 0.0)
    stat_send[...] = jnp.where(left, lse, pltpu.roll(mean, 64, 1))
    stat_g[c] = stat_send[...]
    spread(stat_send, stat_g, "col", 3)
    assemble(qg, qf)
    for h in range(H):
        for t in range(4):
            kbd[TILE * h : TILE * h + TILE, 128 * t : 128 * t + 128] = (
                kf[:, 128 * t : 128 * t + 128] * masks[t][h : h + 1, :]
            ).astype(BF16)

    @pl.loop(0, 32, unroll=8)
    def _(p):
        rows = pl.ds(pl.multiple_of(HP * p, HP), HP)
        e = expo[rows, :]
        terms = []
        for side in (left, jnp.logical_not(left)):
            own = jnp.where(side, e, 0.0)
            terms += [*split(own * dprob[rows, :]), *split(own)]
        res = nn(jnp.concatenate(terms, 0), pp[pl.ds(pl.multiple_of(128 * p, 128), 128), :])
        res = res[:, 0:128] + res[:, 128:256]
        for n in range(4):
            sums_xy[p, n] = res[32 * n : 32 * n + 16] + res[32 * n + 16 : 32 * n + 32]

    wait_recv(stat_g, 3)
    top = stat_g[0]
    for s in range(1, PEERS):
        top = jnp.maximum(top, stat_g[s])
    total = jnp.zeros((HP, 128), F32)
    dsum = jnp.zeros((HP, 128), F32)
    for s in range(PEERS):
        got = stat_g[s]
        weight = jnp.exp(got - top)
        total = total + weight
        dsum = dsum + weight * pltpu.roll(got, 64, 1)
    scales = jnp.exp(row_max - top) / total
    means = dsum / total
    stats[0] = scales
    stats[1] = means

    shifts = scales * means
    w_parts = []
    for p in range(32):
        part = jnp.zeros((HP, 128), F32)
        for odd in range(2):
            i = 2 * p + odd
            part = part + scales[:, i : i + 1] * sums_xy[p, 2 * odd] - shifts[:, i : i + 1] * sums_xy[p, 2 * odd + 1]
        w_parts.append(part)
    while len(w_parts) > 1:
        w_parts = [one + two for one, two in zip(w_parts[0::2], w_parts[1::2])]
    w_send[...] = W_LOGIT * w_parts[0]
    w_row[r] = w_send[...]
    spread(w_send, w_row, "row", 4)

    @pl.loop(0, 8, unroll=8)
    def _(b):
        scale = pltpu.roll(stats[0], lax.rem(128 - 8 * b, 128), 1)
        mean_all = pltpu.roll(stats[1], lax.rem(128 - 8 * b, 128), 1)
        for i in range(4):
            rows = pl.ds(64 * b + 16 * i, 16)
            factor = jnp.where(left, scale[:, 2 * i : 2 * i + 1], scale[:, 2 * i + 1 : 2 * i + 2])
            shift = jnp.where(left, mean_all[:, 2 * i : 2 * i + 1], mean_all[:, 2 * i + 1 : 2 * i + 2])
            p = expo[rows, :] * factor
            ds = p * (dprob[rows, :] - shift)
            high, low = split(ds)
            prob[rows, :] = p.astype(BF16).astype(F32)
            dsr[rows, :] = high.astype(F32)
            dlo[rows, :] = low

    ds_t = jnp.transpose(dsr[...]).astype(BF16)
    prob_t = jnp.transpose(prob[...]).astype(BF16)
    kside = nn(ds_t[0:TILE], qbd[0, :, 0:512]) + nn(ds_t[TILE : 2 * TILE], qbd[1, :, 0:512])
    vside = nn(prob_t[0:TILE], qbd[0, :, 512:1024]) + nn(prob_t[TILE : 2 * TILE], qbd[1, :, 512:1024])
    expand_q = jnp.concatenate((jnp.zeros((64, 256), F32), point_mask, jnp.zeros((48, 256), F32)), 0)
    expand_k = jnp.concatenate((jnp.zeros((80, 256), F32), point_mask, jnp.zeros((32, 256), F32)), 0)
    ps_row = jnp.concatenate(ps_lane, 1)
    kres[:, 0:256] = SCALE_Q * kside[:, 0:256]
    kres[:, 256:512] = -2.0 * ps_row * (
        exact_nn(kside[:, 128:256], expand_q) * kf[:, 256:512] - kside[:, 256:512]
    )
    kres[:, 512:1024] = vside
    for s in range(PEERS):
        for t in range(8):
            kch[s, 4 * t : 4 * t + 4, :] = kres[4 * s : 4 * s + 4, 128 * t : 128 * t + 128]
    kr[r] = kch[r]
    scatter(kch, kr, "row", 5)

    left32 = lax.broadcasted_iota(jnp.int32, (32, 128), 1) < 64
    evens, odds = [], []
    for pairing in range(H // 2):
        one = dsr[pl.ds(2 * pairing, 32, stride=HP), :]
        two = dsr[pl.ds(2 * pairing + 1, 32, stride=HP), :]
        evens.append(jnp.where(left32, one, pltpu.roll(two, 64, 1)).astype(BF16))
        odds.append(jnp.where(left32, pltpu.roll(one, 64, 1), two).astype(BF16))
    lhs = jnp.concatenate((jnp.concatenate(evens, 1), jnp.concatenate(odds, 1)), 0)
    qside = nn(lhs, kbd[...])
    for t in range(4):
        for odd in range(2):
            qres[t, pl.ds(odd, 32, stride=2), :] = qside[32 * odd : 32 * odd + 32, 128 * t : 128 * t + 128]
    row_sums = exact_nn(qres[1], expand_k)
    for t in (2, 3):
        at = 128 * (t - 2)
        qres[t] = -2.0 * ps_lane[t - 2] * (
            row_sums[:, at : at + 128] * qf[:, 128 * t : 128 * t + 128] - qres[t]
        )
    for t in (0, 1):
        qres[t] = SCALE_Q * qres[t]
    for s in range(PEERS):
        for t in range(4):
            qch[s, 4 * t : 4 * t + 4, :] = qres[t, 4 * s : 4 * s + 4, :]
    qr[c] = qch[c]
    scatter(qch, qr, "col", 6)

    wait_recv(w_row, 4)
    w_sum = w_row[0]
    for s in range(1, PEERS):
        w_sum = w_sum + w_row[s]
    w_mid[...] = w_sum
    w_col[c] = w_sum
    spread(w_mid, w_col, "col", 7)

    wb = jnp.concatenate((wb_high, wb_high, wb_low), 0)
    @pl.loop(0, 16, unroll=16)
    def _(t):
        gz = gzp[t]
        for a in range(2):
            rows = pl.ds(32 * t + 16 * a, 16)
            p = prob[rows, :]
            high = dsr[rows, :].astype(BF16)
            lhs = jnp.concatenate(
                (
                    jnp.where(left, p, 0.0).astype(BF16),
                    jnp.where(left, 0.0, p).astype(BF16),
                    high,
                    dlo[rows, :],
                    high,
                ),
                0,
            )
            rhs = jnp.concatenate((gz[32 * a : 32 * a + 32], wb), 0)
            gpair_out[pl.ds(256 * t + 128 * a, 128), :] = tn(lhs, rhs)

    wait_recv(kr, 5)
    ksum = kr[0]
    for s in range(1, PEERS):
        ksum = ksum + kr[s]
    gk_out[:, 0:128] = ksum[0:4]
    gk_out[:, 128:192] = ksum[4:8, 0:64]
    gkp_out[:, 0:128] = ksum[8:12]
    gkp_out[:, 128:144] = ksum[12:16, 0:16]
    gv_out[:, 0:128] = ksum[16:20]
    gv_out[:, 128:192] = ksum[28:32, 0:64]
    gvp_out[:, 0:128] = ksum[20:24]
    gvp_out[:, 128:256] = ksum[24:28]
    gvp_out[:, 256:288] = ksum[28:32, 64:96]
    wait_recv(qr, 6)
    qsum = qr[0]
    for s in range(1, PEERS):
        qsum = qsum + qr[s]
    gq_out[:, 0:128] = qsum[0:4]
    gq_out[:, 128:192] = qsum[4:8, 0:64]
    gqp_out[:, 0:128] = qsum[8:12]
    gqp_out[:, 128:144] = qsum[12:16, 0:16]


    wait_recv(w_col, 7)
    w_sum = w_col[0]
    for s in range(1, PEERS):
        w_sum = w_sum + w_col[s]
    gbw_out[...] = w_sum[0:H]

    for n, dst in enumerate((qg, kg, gzg, stat_g, w_row, kr, qr, w_col)):
        wait_send(dst, n)


def finish(*refs):
    sem = refs[-1]
    pairs = [(refs[n], refs[8 + n]) for n in (6, 0, 1, 2, 3, 4, 5, 7)]
    copies = [pltpu.make_async_copy(src, dst, sem.at[n]) for n, (src, dst) in enumerate(pairs)]
    for copy in copies:
        copy.start()
    for copy in copies:
        copy.wait()


def on_device(
    queries, query_points, key_feats, key_points, values, value_points, pair_rep, bias_weight,
    head_weight, chain_bias, chain_ids, live_mask, cot_scalar, cot_points, cot_pair,
):
    any_spec = pl.BlockSpec(memory_space=pl.ANY)
    vmem_spec = pl.BlockSpec(memory_space=pltpu.VMEM)

    def vm(*shape, kind=F32):
        return pltpu.VMEM(shape, kind)

    scratch = [
        vm(4, 192, kind=BF16), vm(4, 144, kind=BF16), vm(4, 192, kind=BF16), vm(4, 144, kind=BF16),
        vm(4, 192, kind=BF16), vm(4, 288, kind=BF16), vm(4096, 128), vm(H, 128),
        pltpu.SMEM((H,), F32), pltpu.SMEM((H,), F32),
        pltpu.SMEM((8, 128), jnp.int32), pltpu.SMEM((8, 128), jnp.int32),
        vm(8, 128, kind=jnp.int32), vm(8, 128, kind=jnp.int32),
        vm(4, 192, kind=BF16), vm(4, 288, kind=BF16), vm(4, 1536, kind=BF16),
        vm(32, 128), vm(4 * H, 128), vm(32, 128, kind=BF16), vm(32, 128, kind=BF16), vm(4 * H, 128, kind=BF16),
        vm(PEERS, 32, 128, kind=BF16), vm(PEERS, 32, 128, kind=BF16), vm(PEERS, 4 * H, 128, kind=BF16),
        vm(PEERS, 32, 128), vm(PEERS * 4 * H, 128), vm(PEERS * 4 * HP, 128), vm(PEERS, 4 * HP, 128, kind=BF16),
        vm(TILE, 1024), vm(TILE, 1024), vm(1024, 128, kind=BF16), vm(2, 512, 1024, kind=BF16),
        vm(H * TILE, 512, kind=BF16), vm(4096, 256, kind=BF16), vm(16, 256, 256, kind=BF16), vm(32, 4, HP, 128), vm(512, 128), vm(512, 128), vm(512, 128),
        vm(512, 128), vm(512, 128), vm(512, 128), vm(512, 128, kind=BF16),
        vm(3, HP, 128), vm(HP, 128), vm(PEERS, HP, 128), vm(HP, 128), vm(PEERS, HP, 128), vm(HP, 128),
        vm(PEERS, HP, 128),
        vm(TILE, 1024), vm(PEERS, 32, 128), vm(PEERS, 32, 128), vm(4, TILE, 128), vm(PEERS, 16, 128),
        vm(PEERS, 16, 128),
        pltpu.SemaphoreType.DMA((17,)),
        pltpu.SemaphoreType.DMA((8,)), pltpu.SemaphoreType.DMA((8,)),
    ]
    out_shape = [
        jax.ShapeDtypeStruct(shape, F32)
        for shape in ((4, 192), (4, 144), (4, 192), (4, 144), (4, 192), (4, 288), (4096, 128), (H, 128))
    ]
    out = pl.pallas_call(
        kernel,
        out_shape=[pltpu.VMEM(shape.shape, F32) for shape in out_shape],
        in_specs=[any_spec] * 15,
        out_specs=[vmem_spec] * 8,
        scratch_shapes=scratch,
        compiler_params=pltpu.CompilerParams(
            collective_id=0, has_side_effects=True, vmem_limit_bytes=VMEM_LIMIT
        ),
        cost_estimate=pl.CostEstimate(flops=10**9, bytes_accessed=5 * 2**20, transcendentals=10**5),
    )(*(pltpu.with_memory_space_constraint(x, pltpu.HBM) for x in (
        queries, query_points, key_feats, key_points, values, value_points,
        pair_rep.reshape(4096, 128), bias_weight.T, head_weight, chain_bias,
        chain_ids.reshape(8, 128), live_mask.reshape(8, 128), cot_scalar, cot_points, cot_pair,
    )))
    out = pl.pallas_call(
        finish,
        out_shape=out_shape,
        in_specs=[vmem_spec] * 8,
        out_specs=[any_spec] * 8,
        scratch_shapes=[pltpu.SemaphoreType.DMA((8,))],
        compiler_params=pltpu.CompilerParams(vmem_limit_bytes=2**20),
    )(*out)
    return (*out[:6], out[6].reshape(TILE, TILE, 128), out[7].T)


def solution(mesh):
    rc, cr = P(("row", "col"), None), P(("col", "row"), None)
    tile = P("row", "col", None)
    return jax.shard_map(
        on_device,
        mesh=mesh,
        in_specs=(rc, rc, cr, cr, cr, cr, tile, P(), P(), P(), P(), P(), rc, rc, rc),
        out_specs=(rc, rc, cr, cr, cr, cr, tile, P()),
        check_vma=False,
    )
```
